256 devices in a mesh: row: 16 (over y, z_lo), col: 16 (over x, z_hi, core).
Axes of the slice: x: 4, y: 4, z: 8 (z_hi: 2, z_lo: 4; z = z_hi * 4 + z_lo), core: 2. Of those that a mesh axis runs over, the one named last changes fastest.
Arguments:
- pair: bfloat16 [768, 768, 128], P('row', 'col'), may hold values from -6 to 6
- norm_gain: float32 [2, 128], replicated, may hold values from 0.1 to 1.9
- proj_weight: bfloat16 [2, 128, 256], replicated, may hold values from -0.5 to 0.5
- hid_gain: float32 [2, 64], replicated, may hold values from 0.1 to 1.9
- out_weight: bfloat16 [2, 64, 128], replicated, may hold values from -0.75 to 0.75
- gate_weight: bfloat16 [2, 128, 128], replicated, may hold values from -0.5 to 0.5
Outputs:
- updated: bfloat16 [768, 768, 128], P('row', 'col')
The draws below stay inside these ranges and needn't reach their ends.
All inputs are finite; a program needn't handle non-finite values.
Results may differ from the reference program's by a relative error of at most 0.022.
Values may be sent and summed in bfloat16 or wider, within the bound.
No kernel may reach another device: no remote copies, remote signals or barrier semaphores. Data moves between devices by JAX's collectives and lax.ppermute only.
A program may use at most 128 MiB of HBM per device.

```python
import jax
import jax.numpy as jnp
from jax import lax

CP = 128
CH = 64
TOKENS = 768


def block_scale(key, extent, split, least, high):
    loudness, own = 1.0, jax.random.fold_in(key, 6)
    for position, blocks in split:
        steps = jnp.exp(jax.random.uniform(jax.random.fold_in(own, position), (blocks,), jnp.float32, least / len(split), high / len(split)))
        loudness = loudness * jnp.repeat(steps, extent[position] // blocks).reshape([-1 if axis == position else 1 for axis in range(len(extent))])
    return loudness


def scatter_about(stream_key, extent, scale, bound, shards=(), held_as=jnp.bfloat16):
    entries = scale * jax.random.normal(stream_key, extent, jnp.float32)
    if shards:
        entries = entries * block_scale(stream_key, extent, shards, -0.22, 0.18)
    return jnp.clip(entries, -bound, bound).astype(held_as)


def setup_inputs(seed: int = 0) -> dict:
    streams_of = jax.random.split(jax.random.key(seed), 7)
    return {
        "pair": scatter_about(streams_of[0], (TOKENS, TOKENS, CP), 1.0, 6.0, ((0, 16), (1, 16))),
        "norm_gain": jnp.clip(1.0 + 0.18 * jax.random.normal(streams_of[1], (2, CP), jnp.float32), 0.1, 1.9),
        "proj_weight": scatter_about(streams_of[2], (2, CP, 4 * CH), CP ** -0.5, 0.5),
        "hid_gain": jnp.clip(1.0 + 0.18 * jax.random.normal(streams_of[3], (2, CH), jnp.float32), 0.1, 1.9),
        "out_weight": scatter_about(streams_of[4], (2, CH, CP), CH ** -0.5, 0.75),
        "gate_weight": scatter_about(streams_of[5], (2, CP, CP), CP ** -0.5, 0.5),
    }


def layer_norm(values, gain):
    mean = lax.optimization_barrier(jnp.mean(values, axis=-1, keepdims=True))
    centred = values - mean
    var = lax.optimization_barrier(jnp.mean(centred * centred, axis=-1, keepdims=True))
    return centred * jax.lax.rsqrt(var + 1e-05) * gain

def one_pass(block, gain, weight, hgain, oweight, gweight, outgoing):
    normed = layer_norm(block.astype(jnp.float32), gain).astype(jnp.bfloat16)
    proj = jnp.einsum('ijd,de->ije', normed.astype(jnp.float32), weight.astype(jnp.float32))
    width = weight.shape[1] // 4
    left = (jax.nn.sigmoid(proj[..., :width]) * proj[..., width:2 * width]).astype(jnp.bfloat16)
    right = (jax.nn.sigmoid(proj[..., 2 * width:3 * width]) * proj[..., 3 * width:]).astype(jnp.bfloat16)
    left32 = left.astype(jnp.float32)
    right32 = right.astype(jnp.float32)
    if outgoing:
        mixed = jnp.einsum('ikc,jkc->ijc', left32, right32)
    else:
        mixed = jnp.einsum('kic,kjc->ijc', left32, right32)
    hidden = layer_norm(mixed, hgain).astype(jnp.bfloat16)
    gate = jax.nn.sigmoid(jnp.einsum('ijd,de->ije', normed.astype(jnp.float32), gweight.astype(jnp.float32)))
    update = jnp.einsum('ijc,cd->ijd', hidden.astype(jnp.float32), oweight.astype(jnp.float32))
    return (block.astype(jnp.float32) + gate * update).astype(jnp.bfloat16)

def reference(pair, norm_gain, proj_weight, hid_gain, out_weight, gate_weight):
    first = one_pass(pair, norm_gain[0], proj_weight[0], hid_gain[0], out_weight[0], gate_weight[0], True)
    return one_pass(first, norm_gain[1], proj_weight[1], hid_gain[1], out_weight[1], gate_weight[1], False)
```

```python
import functools

import jax
import jax.numpy as jnp
from jax import lax
from jax.experimental import pallas as pl
from jax.experimental.pallas import tpu as pltpu
from jax.sharding import Mesh
from jax.sharding import PartitionSpec as P

F32, BF16 = jnp.float32, jnp.bfloat16
SIDE = 48
HALF = SIDE // 2
SLOT = 64
CH = 64
EPS = 1e-05
NT = (((1,), (1,)), ((), ()))
TN = (((0,), (0,)), ((), ()))
PARAMS = pltpu.CompilerParams(vmem_limit_bytes=56 * 1024 * 1024)
VMEM = pl.BlockSpec(memory_space=pltpu.VMEM)


def call(kernel, outs, n_in, scratch=(), smem=0):
    return pl.pallas_call(
        kernel,
        out_shape=[jax.ShapeDtypeStruct(shape, BF16) for shape in outs],
        in_specs=[VMEM] * n_in + [pl.BlockSpec(memory_space=pltpu.SMEM)] * smem,
        out_specs=[VMEM] * len(outs),
        scratch_shapes=scratch,
        compiler_params=PARAMS,
    )


def low_lanes(rows):
    return lax.broadcasted_iota(jnp.int32, (rows, 2 * SLOT), 1) < SLOT


def pair_up(first, second):
    low = low_lanes(first.shape[0])
    return (
        jnp.where(low, first, pltpu.roll(second, SLOT, 1)),
        jnp.where(low, pltpu.roll(first, SLOT, 1), second),
    )


def layer_norm(values, gain, axis):
    mean = jnp.mean(values, axis=axis, keepdims=True)
    centred = values - mean
    var = jnp.mean(centred * centred, axis=axis, keepdims=True)
    return centred * lax.rsqrt(var + EPS) * gain


def two_rows(ref, s):
    pad = jnp.zeros((SLOT - SIDE, 128), F32)
    return jnp.concatenate([ref[s].astype(F32), pad, ref[s + HALF].astype(F32), pad], axis=0)


def project(rows, s, gain, weight, staged):
    normed = layer_norm(rows, gain, 1).astype(BF16)
    proj = lax.dot_general(weight, normed, NT, preferred_element_type=F32)
    left = jax.nn.sigmoid(proj[:CH]) * proj[CH : 2 * CH]
    right = jax.nn.sigmoid(proj[2 * CH : 3 * CH]) * proj[3 * CH :]
    first, second = pair_up(left, right)
    staged[:, s, :] = first
    staged[:, s + HALF, :] = second


def project_kernel(pair, gain, weight, out, staged):
    wt = weight[...].astype(F32).T.astype(BF16)
    for s in range(HALF):
        project(two_rows(pair, s), s, gain[...], wt, staged)
    out[...] = staged[...].astype(BF16)


def finish(pair, mixed, s, gain, hgain, oweight, gweight):
    rows = two_rows(pair, s)
    normed = layer_norm(rows, gain, 1).astype(BF16)
    gate = jax.nn.sigmoid(jnp.dot(normed, gweight, preferred_element_type=F32))
    hidden = layer_norm(mixed[:, s, :], hgain, 0).astype(BF16)
    update = lax.dot_general(hidden, oweight, TN, preferred_element_type=F32)
    return (rows + gate * update).astype(BF16)


def middle_kernel(pair, mixed, gain, hgain, oweight, gweight, gain2, weight2, z_out, out, mixed32, staged):
    wt = weight2[...].astype(F32).T.astype(BF16)
    hcol = hgain[...].T
    mixed32[...] = mixed[...].astype(F32)
    keep = lax.broadcasted_iota(jnp.int32, (2 * SLOT, 128), 0) % SLOT < SIDE
    for s in range(HALF):
        z = finish(pair, mixed32, s, gain[...], hcol, oweight[...], gweight[...])
        z_out[s] = z[:SIDE]
        z_out[s + HALF] = z[SLOT : SLOT + SIDE]
        rows = jnp.where(keep, z.astype(F32), 0.0)
        project(rows, s, gain2[...], wt, staged)
    out[...] = staged[...].astype(BF16)


def last_kernel(pair, mixed, gain, hgain, oweight, gweight, z_out, mixed32):
    hcol = hgain[...].T
    mixed32[...] = mixed[...].astype(F32)
    for s in range(HALF):
        z = finish(pair, mixed32, s, gain[...], hcol, oweight[...], gweight[...])
        z_out[s] = z[:SIDE]
        z_out[s + HALF] = z[SLOT : SLOT + SIDE]


def lanes_of(ref, which, base):
    return jnp.concatenate([ref[p][:, base : base + SIDE] for p in which], axis=1)


def split_out_kernel(got, left, right):
    for a in range(4):
        rows = slice(a * SIDE, (a + 1) * SIDE)
        which = range(a * 16, a * 16 + 16)
        left[rows, :] = lanes_of(got, which, 0)
        right[rows, :] = lanes_of(got, which, SLOT)


def send_back(total, place, out):
    for a in range(4):
        for b in range(0, 4, 2):
            tile = total[a * SIDE : (a + 1) * SIDE, b * SLOT : (b + 2) * SLOT]
            first, second = pair_up(tile[:HALF], tile[HALF:])
            out[place(a, b)] = first.astype(BF16)
            out[place(a, b + 1)] = second.astype(BF16)


def mix_out_kernel(left, r0, r1, r2, r3, me, out):
    pad = jnp.zeros((SLOT - SIDE, 768), BF16)
    for step, ref in enumerate((r0, r1, r2, r3)):
        pieces = []
        for b in range(4):
            pieces += [ref[b * SIDE : (b + 1) * SIDE, :], pad]
        total = lax.dot_general(left[...], jnp.concatenate(pieces, axis=0), NT, preferred_element_type=F32)
        owner = lax.rem(me[0] + step, 4)
        send_back(total, lambda a, b: a * 16 + owner * 4 + b, out)


def split_in_kernel(got, left, right):
    for r in range(8):
        rows = slice(r * SIDE, (r + 1) * SIDE)
        which = list(range(r * 4, r * 4 + 4)) + list(range((r + 8) * 4, (r + 8) * 4 + 4))
        left[rows, :] = lanes_of(got, which, 0)
    for r in range(16):
        for b in range(0, 4, 2):
            first, second = got[r * 4 + b].astype(F32), got[r * 4 + b + 1].astype(F32)
            low = low_lanes(SIDE)
            tile = jnp.where(low, pltpu.roll(first, SLOT, 1), second)
            right[r * SIDE : (r + 1) * SIDE, b * SLOT : (b + 2) * SLOT] = tile.astype(BF16)


def mix_in_kernel(right, l0, l1, l2, l3, me, out):
    for step, ref in enumerate((l0, l1, l2, l3)):
        total = lax.dot_general(
            ref[:, :192], right[:384, :], TN, preferred_element_type=F32
        ) + lax.dot_general(ref[:, 192:], right[384:, :], TN, preferred_element_type=F32)
        owner = lax.rem(me[0] + step, 4)
        send_back(total, lambda a, b: owner * 16 + a * 4 + b, out)


def around(values, axis):
    return [values] + [
        lax.ppermute(values, axis, [((i + step) % 4, i) for i in range(4)]) for step in (1, 2, 3)
    ]


MESSAGE = (64, SIDE, 128)
BACK = (64, HALF, 128)
BLOCK = (SIDE, SIDE, 128)


def body(pair, norm_gain, proj_weight, hid_gain, out_weight, gate_weight):
    staged = pltpu.VMEM(MESSAGE, F32)
    mixed32 = pltpu.VMEM(BACK, F32)
    gain = [norm_gain[p : p + 1] for p in range(2)]
    hgain = [hid_gain[p : p + 1] for p in range(2)]
    out_axes, in_axes = ("zl", "x", "zh", "c"), ("y", "zl", "zh", "c")

    (sent,) = call(project_kernel, [MESSAGE], 3, [staged])(pair, gain[0], proj_weight[0])
    got = lax.all_to_all(sent, out_axes, 0, 0, tiled=True)
    left, right = call(split_out_kernel, [(192, 768)] * 2, 1)(got)
    me = lax.axis_index("y").reshape(1)
    (sent,) = call(mix_out_kernel, [BACK], 5, smem=1)(left, *around(right, "y"), me)
    mixed = lax.all_to_all(sent, out_axes, 0, 0, tiled=True)
    first, sent = call(middle_kernel, [BLOCK, MESSAGE], 8, [mixed32, staged])(
        pair, mixed, gain[0], hgain[0], out_weight[0], gate_weight[0], gain[1], proj_weight[1]
    )
    got = lax.all_to_all(sent, in_axes, 0, 0, tiled=True)
    left, right = call(split_in_kernel, [(384, 384), (768, 256)], 1)(got)
    me = lax.axis_index("x").reshape(1)
    (sent,) = call(mix_in_kernel, [BACK], 5, smem=1)(right, *around(left, "x"), me)
    mixed = lax.all_to_all(sent, in_axes, 0, 0, tiled=True)
    (updated,) = call(last_kernel, [BLOCK], 6, [mixed32])(
        first, mixed, gain[1], hgain[1], out_weight[1], gate_weight[1]
    )
    return updated


def solution(mesh):
    fine = Mesh(mesh.devices.reshape(4, 4, 4, 2, 2), ("y", "zl", "x", "zh", "c"))
    spec = P(("y", "zl"), ("x", "zh", "c"), None)
    return jax.shard_map(
        body,
        mesh=fine,
        in_specs=(spec, P(), P(), P(), P(), P()),
        out_specs=spec,
        check_vma=False,
    )
```

```python
import jax
import jax.numpy as jnp
from jax import lax
from jax.experimental import pallas as pl
from jax.experimental.pallas import tpu as pltpu
from jax.sharding import Mesh
from jax.sharding import PartitionSpec as P

F32, BF16 = jnp.float32, jnp.bfloat16
SIDE = 48
HALF = SIDE // 2
SLOT = 64
MAIN = 40
EXTRA = SIDE - MAIN
PIECE = 16
CH = 64
LANES = 128
EPS = 1e-05
NT = (((1,), (1,)), ((), ()))
TN = (((0,), (0,)), ((), ()))
VMEM = pl.BlockSpec(memory_space=pltpu.VMEM)
SMEM = pl.BlockSpec(memory_space=pltpu.SMEM)


def call(kernel, outs, n_in, scratch=(), smem=0):
    return pl.pallas_call(
        kernel,
        out_shape=[jax.ShapeDtypeStruct(shape, BF16) for shape in outs],
        in_specs=[VMEM] * n_in + [SMEM] * smem,
        out_specs=[VMEM] * len(outs),
        scratch_shapes=scratch,
        compiler_params=pltpu.CompilerParams(vmem_limit_bytes=16 * 1024 * 1024),
    )


def lane_of(rows):
    return lax.broadcasted_iota(jnp.int32, (rows, LANES), 1)


def layer_norm(values, gain, axis):
    mean = jnp.mean(values, axis=axis, keepdims=True)
    centred = values - mean
    var = jnp.mean(centred * centred, axis=axis, keepdims=True)
    return centred * lax.rsqrt(var + EPS) * gain


def sigmoid(values):
    return 0.5 * jnp.tanh(0.5 * values) + 0.5


def two_rows(ref, s):
    pad = jnp.zeros((SLOT - SIDE, LANES), F32)
    return jnp.concatenate([ref[s].astype(F32), pad, ref[s + HALF].astype(F32), pad], axis=0)


def project(rows, s, gain, weight, staged, extra):
    normed = layer_norm(rows, gain, 1).astype(BF16)
    proj = lax.dot_general(weight, normed, NT, preferred_element_type=F32)
    left = sigmoid(proj[:CH]) * proj[CH : 2 * CH]
    right = sigmoid(proj[2 * CH : 3 * CH]) * proj[3 * CH :]
    lane = lane_of(CH)
    first = jnp.where(lane < SIDE, left, pltpu.roll(right, SIDE, 1))
    second = jnp.where(lane < SIDE, pltpu.roll(left, SLOT, 1), pltpu.roll(right, LANES + SIDE - SLOT, 1))
    if s + HALF >= MAIN:
        for g in range(SIDE // PIECE):
            moved = jnp.where(
                lane < 2 * SIDE + PIECE,
                pltpu.roll(second, 2 * SIDE - g * PIECE, 1),
                pltpu.roll(second, SIDE + PIECE - g * PIECE, 1),
            )
            extra[g * EXTRA + s + HALF - MAIN] = moved
    else:
        staged[pl.ds((s + HALF) * CH, CH), :] = second
    staged[pl.ds(s * CH, CH), :] = jnp.where(lane < 2 * SIDE, first, extra[s])


ORDER = [*range(HALF - EXTRA, HALF), *range(HALF - EXTRA)]


def write_messages(staged, out):
    for channel in range(CH):
        out[channel] = staged[pl.ds(channel, MAIN, stride=CH), :].astype(BF16)


def project_kernel(pair, gain, weight, out, staged, extra):
    wt = weight[0].astype(F32).T.astype(BF16)
    for s in ORDER:
        project(two_rows(pair, s), s, gain[0:1, :], wt, staged, extra)
    write_messages(staged, out)


def finish(pair, mixed, s, gain, hgain, oweight, gweight):
    rows = two_rows(pair, s)
    normed = layer_norm(rows, gain, 1).astype(BF16)
    gate = sigmoid(jnp.dot(normed, gweight, preferred_element_type=F32))
    sums = mixed[pl.ds(s, CH, stride=HALF), :]
    hidden = layer_norm(sums, hgain, 0).astype(BF16)
    update = lax.dot_general(hidden, oweight, TN, preferred_element_type=F32)
    return (rows + gate * update).astype(BF16)


def read_sums(mixed, mixed32):
    for channel in range(CH):
        mixed32[pl.ds(channel * HALF, HALF), :] = mixed[channel].astype(F32)


def middle_kernel(pair, mixed, gain, hgain, oweight, gweight, weight, z_out, out, mixed32, staged, extra):
    wt = weight[1].astype(F32).T.astype(BF16)
    hcol = hgain[...].T[:, 0:1]
    read_sums(mixed, mixed32)
    keep = lax.broadcasted_iota(jnp.int32, (2 * SLOT, LANES), 0) % SLOT < SIDE
    for s in ORDER:
        z = finish(pair, mixed32, s, gain[0:1, :], hcol, oweight[0], gweight[0])
        z_out[s] = z[:SIDE]
        z_out[s + HALF] = z[SLOT : SLOT + SIDE]
        rows = jnp.where(keep, z.astype(F32), 0.0)
        project(rows, s, gain[1:2, :], wt, staged, extra)
    write_messages(staged, out)


def last_kernel(pair, mixed, gain, hgain, oweight, gweight, z_out, mixed32):
    hcol = hgain[...].T[:, 1:2]
    read_sums(mixed, mixed32)
    for s in range(HALF):
        z = finish(pair, mixed32, s, gain[1:2, :], hcol, oweight[1], gweight[1])
        z_out[s] = z[:SIDE]
        z_out[s + HALF] = z[SLOT : SLOT + SIDE]


def block_of(ref, p, base):
    values = ref[p].astype(F32)
    start = 2 * SIDE + (PIECE if base else 0)
    tail = [values[g * EXTRA : (g + 1) * EXTRA, start : start + PIECE] for g in range(SIDE // PIECE)]
    return jnp.concatenate([values[:, base : base + SIDE], jnp.concatenate(tail, axis=1)], axis=0)


def blocks_of(ref, which, base):
    return jnp.concatenate([block_of(ref, p, base) for p in which], axis=1).astype(BF16)


def split_out_kernel(got, me, left, kept, given):
    for a in range(8):
        left[a * SIDE : (a + 1) * SIDE, :] = blocks_of(got, [a * 8 + b for b in range(8)], 0)
    for a in range(4):
        rows = slice(a * SIDE, (a + 1) * SIDE)
        mine, other = (2 * a + me[0]) * 8, (2 * a + 1 - me[0]) * 8
        kept[rows, :] = blocks_of(got, [mine + b for b in range(8)], SIDE)
        given[rows, :] = blocks_of(got, [other + b for b in range(8)], SIDE)


def send_back(total, blocks, place, out):
    lane = lane_of(HALF)
    for a in range(blocks):
        for b in range(0, 4, 2):
            tile = total[a * SIDE : (a + 1) * SIDE, b * SLOT : (b + 2) * SLOT]
            low, high = tile[:HALF], tile[HALF:]
            out[place(a, b)] = jnp.where(lane < SLOT, low, pltpu.roll(high, SLOT, 1)).astype(BF16)
            out[place(a, b + 1)] = jnp.where(lane < SLOT, pltpu.roll(low, SLOT, 1), high).astype(BF16)


def padded(ref):
    pad = jnp.zeros((SLOT - SIDE, ref.shape[1]), BF16)
    pieces = []
    for b in range(4):
        pieces += [ref[b * SIDE : (b + 1) * SIDE, :], pad]
    return jnp.concatenate(pieces, axis=0)


def mix_out_kernel(left, left_c, kept, given_c, kept_y, given_d, me, out):
    for step, (near, far) in enumerate(((kept, given_c), (kept_y, given_d))):
        total = lax.dot_general(left[...], padded(near), NT, preferred_element_type=F32)
        total += lax.dot_general(left_c[...], padded(far), NT, preferred_element_type=F32)
        owner = me[0] if step == 0 else 1 - me[0]
        send_back(total, 8, lambda a, b: a * 8 + (2 * (b // 2) + owner) * 2 + b % 2, out)


def split_in_kernel(got, left, right):
    for r in range(8):
        rows = slice(r * SIDE, (r + 1) * SIDE)
        left[rows, :] = blocks_of(got, [(r + 8 * h) * 4 + b for h in range(2) for b in range(4)], 0)
    pad = jnp.zeros((SIDE, SLOT - SIDE), F32)
    for r in range(16):
        pieces = []
        for b in range(4):
            pieces += [block_of(got, r * 4 + b, SIDE), pad]
        right[r * SIDE : (r + 1) * SIDE, :] = jnp.concatenate(pieces, axis=1).astype(BF16)


def mix_in_kernel(right, left, left_c, left_x, left_d, me, out):
    for step, ref in enumerate((left, left_c, left_x, left_d)):
        total = lax.dot_general(ref[:, :192], right[:384, :], TN, preferred_element_type=F32)
        total += lax.dot_general(ref[:, 192:], right[384:, :], TN, preferred_element_type=F32)
        core = me[1] if step % 2 == 0 else 1 - me[1]
        low = me[0] if step < 2 else 1 - me[0]
        send_back(
            total,
            4,
            lambda a, b: (2 * (a // 2) + low) * 16 + (2 * (a % 2) + core) * 4 + b,
            out,
        )


def swap(values, *axes):
    n = 1 << len(axes)
    return lax.ppermute(values, axes, [(i, n - 1 - i) for i in range(n)])


MESSAGE = (CH, MAIN, LANES)
BACK = (CH, HALF, LANES)
BLOCK = (SIDE, SIDE, LANES)


def body(pair, norm_gain, proj_weight, hid_gain, out_weight, gate_weight):
    staged = pltpu.VMEM((MAIN * CH, LANES), F32)
    extra = pltpu.VMEM((HALF, CH, LANES), F32)
    mixed32 = pltpu.VMEM((CH * HALF, LANES), F32)
    out_axes, in_axes = ("yh", "zl", "xh", "xl", "zh"), ("yh", "yl", "zl", "xh", "zh")
    core = lax.axis_index("c")

    (sent,) = call(project_kernel, [MESSAGE], 3, [staged, extra])(pair, norm_gain, proj_weight)
    got = lax.all_to_all(sent, out_axes, 0, 0, tiled=True)
    left, kept, given = call(split_out_kernel, [(384, 384), (192, 384), (192, 384)], 1, smem=1)(
        got, core.reshape(1)
    )
    (sent,) = call(mix_out_kernel, [BACK], 6, smem=1)(
        left,
        swap(left, "c"),
        kept,
        swap(given, "c"),
        swap(kept, "yl"),
        swap(given, "yl", "c"),
        lax.axis_index("yl").reshape(1),
    )
    mixed = lax.all_to_all(sent, out_axes, 0, 0, tiled=True)
    first, sent = call(middle_kernel, [BLOCK, MESSAGE], 7, [mixed32, staged, extra])(
        pair, mixed, norm_gain, hid_gain, out_weight, gate_weight, proj_weight
    )
    got = lax.all_to_all(sent, in_axes, 0, 0, tiled=True)
    left, right = call(split_in_kernel, [(384, 384), (768, 256)], 1)(got)
    (sent,) = call(mix_in_kernel, [BACK], 5, smem=1)(
        right,
        left,
        swap(left, "c"),
        swap(left, "xl"),
        swap(left, "xl", "c"),
        jnp.stack([lax.axis_index("xl"), core]),
    )
    mixed = lax.all_to_all(sent, in_axes, 0, 0, tiled=True)
    (updated,) = call(last_kernel, [BLOCK], 6, [mixed32])(
        first, mixed, norm_gain, hid_gain, out_weight, gate_weight
    )
    return updated


def solution(mesh):
    names = ("yh", "yl", "zl", "xh", "xl", "zh", "c")
    fine = Mesh(mesh.devices.reshape(2, 2, 4, 2, 2, 2, 2), names)
    spec = P(names[:3], names[3:], None)
    return jax.shard_map(
        body,
        mesh=fine,
        in_specs=(spec, P(), P(), P(), P(), P()),
        out_specs=spec,
        check_vma=False,
    )
```

```python
import jax
import jax.numpy as jnp
from jax import lax
from jax.experimental import pallas as pl
from jax.experimental.pallas import tpu as pltpu
from jax.sharding import Mesh
from jax.sharding import PartitionSpec as P

F32, BF16 = jnp.float32, jnp.bfloat16
SIDE = 48
HALF = SIDE // 2
SLOT = 64
MAIN = 40
EXTRA = SIDE - MAIN
STRIDE = 72
GROUP = 8
PIECE = 16
CH = 64
LANES = 128
EPS = 1e-05
NT = (((1,), (1,)), ((), ()))
TN = (((0,), (0,)), ((), ()))
VMEM = pl.BlockSpec(memory_space=pltpu.VMEM)
SMEM = pl.BlockSpec(memory_space=pltpu.SMEM)


def call(kernel, outs, n_in, scratch=(), smem=0):
    return pl.pallas_call(
        kernel,
        out_shape=[jax.ShapeDtypeStruct(shape, BF16) for shape in outs],
        in_specs=[VMEM] * n_in + [SMEM] * smem,
        out_specs=[VMEM] * len(outs),
        scratch_shapes=scratch,
        compiler_params=pltpu.CompilerParams(vmem_limit_bytes=16 * 1024 * 1024),
    )


def lane_of(rows):
    return lax.broadcasted_iota(jnp.int32, (rows, LANES), 1)


def layer_norm(values, gain, axis):
    mean = jnp.mean(values, axis=axis, keepdims=True)
    centred = values - mean
    var = jnp.mean(centred * centred, axis=axis, keepdims=True)
    return centred * lax.rsqrt(var + EPS) * gain


def sigmoid(values):
    return 0.5 * jnp.tanh(0.5 * values) + 0.5


def normalize(block, gain, normed):
    pad = jnp.zeros((SLOT - SIDE, LANES), BF16)
    for start in range(0, SIDE, GROUP):
        rows = layer_norm(block[start : start + GROUP].astype(F32), gain.reshape(1, 1, LANES), 2)
        rows = rows.astype(BF16)
        for i in range(GROUP):
            base = place_of(start + i)
            normed[base : base + SIDE, :] = rows[i]
            normed[base + SIDE : base + SLOT, :] = pad


def place_of(i):
    return (i % HALF) * LANES + (i // HALF) * SLOT


def project(normed, weight, staged, extra):
    wt = weight.astype(F32).T.astype(BF16)
    lane = lane_of(CH)
    for s in ORDER:
        proj = lax.dot_general(wt, normed[s * LANES : (s + 1) * LANES, :], NT, preferred_element_type=F32)
        left = sigmoid(proj[:CH]) * proj[CH : 2 * CH]
        right = sigmoid(proj[2 * CH : 3 * CH]) * proj[3 * CH :]
        first = jnp.where(lane < SLOT, left, pltpu.roll(right, SLOT, 1))
        second = jnp.where(lane < SLOT, pltpu.roll(left, SLOT, 1), right)
        if s + HALF >= MAIN:
            for g in range(SIDE // PIECE):
                extra[g * EXTRA + s + HALF - MAIN] = pltpu.roll(second, SIDE - g * PIECE, 1)
        else:
            staged[pl.ds((s + HALF) * STRIDE, CH), :] = second
        staged[pl.ds(s * STRIDE, CH), :] = jnp.where(lane % SLOT < SIDE, first, extra[s])


ORDER = [*range(HALF - EXTRA, HALF), *range(HALF - EXTRA)]


def write_messages(staged, out):
    for channel in range(CH):
        out[channel] = staged[pl.ds(channel, MAIN, stride=STRIDE), :].astype(BF16)


def project_kernel(pair, gain, weight, out, normed, staged, extra):
    normalize(pair, gain[0:1, :], normed)
    project(normed, weight[0], staged, extra)
    write_messages(staged, out)


def read_sums(mixed, mixed32):
    for channel in range(CH):
        mixed32[pl.ds(channel * HALF, HALF), :] = mixed[channel].astype(F32)


def finish(pair, normed, mixed, hgain, oweight, gweight, z_out, mixed32, hidden):
    hcol = hgain.T
    read_sums(mixed, mixed32)
    for s in range(0, HALF, 4):
        sums = [mixed32[pl.ds(s + t, CH, stride=HALF), :] for t in range(4)]
        sums = [layer_norm(values, hcol, 0).astype(BF16) for values in sums]
        for t in range(4):
            hidden[s + t] = sums[t]
    for s in range(0, HALF, 4):
        rows = slice(s * LANES, (s + 4) * LANES)
        gate = sigmoid(jnp.dot(normed[rows, :], gweight, preferred_element_type=F32))
        updates = [
            lax.dot_general(hidden[s + t], oweight, TN, preferred_element_type=F32) for t in range(4)
        ]
        change = gate * jnp.concatenate(updates, axis=0)
        for h in range(2):
            old = [pair[s + t + h * HALF].astype(F32) for t in range(4)]
            new = [
                old[t] + change[t * LANES + h * SLOT : t * LANES + h * SLOT + SIDE] for t in range(4)
            ]
            for t in range(4):
                z_out[s + t + h * HALF] = new[t].astype(BF16)


def middle_kernel(
    pair, mixed, gain, hgain, oweight, gweight, weight, z_out, out, normed, mixed32, hidden, staged, extra
):
    normalize(pair, gain[0:1, :], normed)
    finish(pair, normed, mixed, hgain[0:1, :], oweight[0], gweight[0], z_out, mixed32, hidden)
    normalize(z_out, gain[1:2, :], normed)
    project(normed, weight[1], staged, extra)
    write_messages(staged, out)


def last_kernel(pair, mixed, gain, hgain, oweight, gweight, z_out, normed, mixed32, hidden):
    normalize(pair, gain[1:2, :], normed)
    finish(pair, normed, mixed, hgain[1:2, :], oweight[1], gweight[1], z_out, mixed32, hidden)


def moved(ref, p, base, offset):
    values = ref[p].astype(F32)
    lane = lane_of(EXTRA)
    tail = None
    for g in range(SIDE // PIECE):
        begin = offset + g * PIECE
        part = values[g * EXTRA : (g + 1) * EXTRA]
        shift = (begin - base - SIDE) % LANES
        part = pltpu.roll(part, shift, 1) if shift else part
        tail = part if tail is None else jnp.where((lane - begin) % LANES < PIECE, part, tail)
    shift = (offset - base) % LANES
    main = pltpu.roll(values, shift, 1) if shift else values
    return jnp.concatenate([main, tail], axis=0)


def dense(ref, which, base):
    lane = lane_of(SIDE)
    tiles = [None] * 3
    for b, p in enumerate(which):
        first, offset = divmod(b * SIDE, LANES)
        block = moved(ref, p, base, offset)
        tiles[first] = block if offset == 0 else jnp.where(lane < offset, tiles[first], block)
        if offset + SIDE > LANES:
            tiles[first + 1] = block
    return jnp.concatenate(tiles, axis=1).astype(BF16)


def split_out_kernel(got, me, left, kept, given):
    for a in range(8):
        left[a * SIDE : (a + 1) * SIDE, :] = dense(got, [a * 8 + b for b in range(8)], 0)
    for a in range(4):
        rows = slice(a * SIDE, (a + 1) * SIDE)
        mine, other = (2 * a + me[0]) * 8, (2 * a + 1 - me[0]) * 8
        kept[rows, :] = dense(got, [mine + b for b in range(8)], SLOT)
        given[rows, :] = dense(got, [other + b for b in range(8)], SLOT)


def send_back(total, blocks, place, out):
    lane = lane_of(HALF)
    for a in range(blocks):
        for b in range(0, 4, 2):
            tile = total[a * SIDE : (a + 1) * SIDE, b * SLOT : (b + 2) * SLOT]
            low, high = tile[:HALF], tile[HALF:]
            out[place(a, b)] = jnp.where(lane < SLOT, low, pltpu.roll(high, SLOT, 1)).astype(BF16)
            out[place(a, b + 1)] = jnp.where(lane < SLOT, pltpu.roll(low, SLOT, 1), high).astype(BF16)


def padded(ref):
    pad = jnp.zeros((SLOT - SIDE, ref.shape[1]), BF16)
    pieces = []
    for b in range(4):
        pieces += [ref[b * SIDE : (b + 1) * SIDE, :], pad]
    return jnp.concatenate(pieces, axis=0)


def mix_out_kernel(left, left_c, kept, given_c, kept_y, given_d, me, out):
    for step, (near, far) in enumerate(((kept, given_c), (kept_y, given_d))):
        total = lax.dot_general(left[...], padded(near), NT, preferred_element_type=F32)
        total += lax.dot_general(left_c[...], padded(far), NT, preferred_element_type=F32)
        owner = me[0] if step == 0 else 1 - me[0]
        send_back(total, 8, lambda a, b: a * 8 + (2 * (b // 2) + owner) * 2 + b % 2, out)


def split_in_kernel(got, left, right):
    for r in range(8):
        rows = slice(r * SIDE, (r + 1) * SIDE)
        left[rows, :] = dense(got, [(r + 8 * h) * 4 + b for h in range(2) for b in range(4)], 0)
    lane = lane_of(SIDE)
    for r in range(16):
        for b in range(0, 4, 2):
            low, high = moved(got, r * 4 + b, SLOT, 0), moved(got, r * 4 + b + 1, SLOT, SLOT)
            tile = jnp.where(lane < SLOT, low, high)
            right[r * SIDE : (r + 1) * SIDE, b * SLOT : (b + 2) * SLOT] = tile.astype(BF16)


def mix_in_kernel(right, left, left_c, left_x, left_d, me, out):
    for step, ref in enumerate((left, left_c, left_x, left_d)):
        total = lax.dot_general(ref[:, :192], right[:384, :], TN, preferred_element_type=F32)
        total += lax.dot_general(ref[:, 192:], right[384:, :], TN, preferred_element_type=F32)
        core = me[1] if step % 2 == 0 else 1 - me[1]
        low = me[0] if step < 2 else 1 - me[0]
        send_back(
            total,
            4,
            lambda a, b: (2 * (a // 2) + low) * 16 + (2 * (a % 2) + core) * 4 + b,
            out,
        )


def swap(values, *axes):
    n = 1 << len(axes)
    return lax.ppermute(values, axes, [(i, n - 1 - i) for i in range(n)])


MESSAGE = (CH, MAIN, LANES)
BACK = (CH, HALF, LANES)
BLOCK = (SIDE, SIDE, LANES)


def body(pair, norm_gain, proj_weight, hid_gain, out_weight, gate_weight):
    normed = pltpu.VMEM((HALF * LANES, LANES), BF16)
    staged = pltpu.VMEM((MAIN * STRIDE, LANES), F32)
    extra = pltpu.VMEM((HALF, CH, LANES), F32)
    mixed32 = pltpu.VMEM((CH * HALF, LANES), F32)
    hidden = pltpu.VMEM((HALF, CH, LANES), BF16)
    out_axes, in_axes = ("yh", "zl", "xh", "xl", "zh"), ("yh", "yl", "zl", "xh", "zh")
    core = lax.axis_index("c")

    (sent,) = call(project_kernel, [MESSAGE], 3, [normed, staged, extra])(pair, norm_gain, proj_weight)
    got = lax.all_to_all(sent, out_axes, 0, 0, tiled=True)
    left, kept, given = call(split_out_kernel, [(384, 384), (192, 384), (192, 384)], 1, smem=1)(
        got, core.reshape(1)
    )
    (sent,) = call(mix_out_kernel, [BACK], 6, smem=1)(
        left,
        swap(left, "c"),
        kept,
        swap(given, "c"),
        swap(kept, "yl"),
        swap(given, "yl", "c"),
        lax.axis_index("yl").reshape(1),
    )
    mixed = lax.all_to_all(sent, out_axes, 0, 0, tiled=True)
    first, sent = call(middle_kernel, [BLOCK, MESSAGE], 7, [normed, mixed32, hidden, staged, extra])(
        pair, mixed, norm_gain, hid_gain, out_weight, gate_weight, proj_weight
    )
    got = lax.all_to_all(sent, in_axes, 0, 0, tiled=True)
    left, right = call(split_in_kernel, [(384, 384), (768, 256)], 1)(got)
    left_x = swap(left, "xl")
    (sent,) = call(mix_in_kernel, [BACK], 5, smem=1)(
        right,
        left,
        swap(left, "c"),
        left_x,
        swap(left_x, "c"),
        jnp.stack([lax.axis_index("xl"), core]),
    )
    mixed = lax.all_to_all(sent, in_axes, 0, 0, tiled=True)
    (updated,) = call(last_kernel, [BLOCK], 6, [normed, mixed32, hidden])(
        first, mixed, norm_gain, hid_gain, out_weight, gate_weight
    )
    return updated


def solution(mesh):
    names = ("yh", "yl", "zl", "xh", "xl", "zh", "c")
    fine = Mesh(mesh.devices.reshape(2, 2, 4, 2, 2, 2, 2), names)
    spec = P(names[:3], names[3:], None)
    return jax.shard_map(
        body,
        mesh=fine,
        in_specs=(spec, P(), P(), P(), P(), P()),
        out_specs=spec,
        check_vma=False,
    )
```

```python
import functools

import jax
import jax.numpy as jnp
from jax import lax
from jax.experimental import pallas as pl
from jax.experimental.pallas import tpu as pltpu
from jax.sharding import Mesh
from jax.sharding import PartitionSpec as P

F32, BF16 = jnp.float32, jnp.bfloat16
SIDE = 48
HALF = SIDE // 2
SLOT = 64
MAIN = 40
EXTRA = SIDE - MAIN
STRIDE = 72
GROUP = 8
PIECE = 16
CH = 64
LANES = 128
EPS = 1e-05
NT = (((1,), (1,)), ((), ()))
TN = (((0,), (0,)), ((), ()))
VMEM = pl.BlockSpec(memory_space=pltpu.VMEM)
SMEM = pl.BlockSpec(memory_space=pltpu.SMEM)
HBM = pl.BlockSpec(memory_space=pltpu.HBM)


def call(kernel, outs, n_in, scratch=(), smem=0, inputs=VMEM, outputs=VMEM, dtype=BF16, limit=16 << 20):
    return pl.pallas_call(
        kernel,
        out_shape=[jax.ShapeDtypeStruct(shape, dtype) for shape in outs],
        in_specs=[inputs] * n_in + [SMEM] * smem,
        out_specs=[outputs] * len(outs),
        scratch_shapes=scratch,
        compiler_params=pltpu.CompilerParams(vmem_limit_bytes=limit),
    )


def lane_of(rows):
    return lax.broadcasted_iota(jnp.int32, (rows, LANES), 1)


def layer_norm(values, gain, axis):
    mean = jnp.mean(values, axis=axis, keepdims=True)
    centred = values - mean
    var = jnp.mean(centred * centred, axis=axis, keepdims=True)
    return centred * lax.rsqrt(var + EPS) * gain


def sigmoid(values):
    return 0.5 * jnp.tanh(0.5 * values) + 0.5


def normalize(block, gain, normed, arrive=lambda start: None):
    pad = jnp.zeros((SLOT - SIDE, LANES), BF16)
    for start in range(0, SIDE, GROUP):
        arrive(start)
        rows = layer_norm(block[start : start + GROUP].astype(F32), gain.reshape(1, 1, LANES), 2)
        rows = rows.astype(BF16)
        for i in range(GROUP):
            base = place_of(start + i)
            normed[base : base + SIDE, :] = rows[i]
            normed[base + SIDE : base + SLOT, :] = pad


def place_of(i):
    return (i % HALF) * LANES + (i // HALF) * SLOT


def project(normed, weight, staged, extra):
    wt = weight.astype(F32).T.astype(BF16)
    lane = lane_of(CH)
    for s in ORDER:
        proj = lax.dot_general(wt, normed[s * LANES : (s + 1) * LANES, :], NT, preferred_element_type=F32)
        left = sigmoid(proj[:CH]) * proj[CH : 2 * CH]
        right = sigmoid(proj[2 * CH : 3 * CH]) * proj[3 * CH :]
        first = jnp.where(lane < SLOT, left, pltpu.roll(right, SLOT, 1))
        second = jnp.where(lane < SLOT, pltpu.roll(left, SLOT, 1), right)
        if s + HALF >= MAIN:
            for g in range(SIDE // PIECE):
                extra[g * EXTRA + s + HALF - MAIN] = pltpu.roll(second, SIDE - g * PIECE, 1)
        else:
            staged[pl.ds((s + HALF) * STRIDE, CH), :] = second
        staged[pl.ds(s * STRIDE, CH), :] = jnp.where(lane % SLOT < SIDE, first, extra[s])


ORDER = [*range(HALF - EXTRA, HALF), *range(HALF - EXTRA)]


def write_messages(staged, out):
    for channel in range(CH):
        out[channel] = staged[pl.ds(channel, MAIN, stride=STRIDE), :].astype(BF16)


def project_kernel(pair_hbm, gain_hbm, weight_hbm, out, pair, gain, weight, sems, normed, staged, extra):
    groups = SIDE // GROUP
    copies = [pltpu.make_async_copy(gain_hbm, gain, sems.at[groups])]
    for n in range(groups):
        rows = pl.ds(n * GROUP, GROUP)
        copies.append(pltpu.make_async_copy(pair_hbm.at[rows], pair.at[rows], sems.at[n]))
    copies.append(pltpu.make_async_copy(weight_hbm.at[0], weight, sems.at[groups + 1]))
    for copy in copies:
        copy.start()
    copies[0].wait()
    normalize(pair, gain[0:1, :], normed, lambda start: copies[1 + start // GROUP].wait())
    copies[-1].wait()
    project(normed, weight[...], staged, extra)
    write_messages(staged, out)


def gate_kernel(p, pair, gain, gweight, gate, normed):
    normalize(pair, gain[p : p + 1, :], normed)
    for start in range(0, HALF * LANES, 4 * LANES):
        rows = slice(start, start + 4 * LANES)
        gate[rows, :] = sigmoid(jnp.dot(normed[rows, :], gweight[p], preferred_element_type=F32))


def read_sums(mixed, mixed32):
    for channel in range(CH):
        mixed32[pl.ds(channel * HALF, HALF), :] = mixed[channel].astype(F32)


def finish(pair, gate, mixed, hgain, oweight, z_out, mixed32, hidden, ready=lambda s: None):
    hcol = hgain.T
    read_sums(mixed, mixed32)
    for s in range(0, HALF, 4):
        sums = [mixed32[pl.ds(s + t, CH, stride=HALF), :] for t in range(4)]
        sums = [layer_norm(values, hcol, 0).astype(BF16) for values in sums]
        for t in range(4):
            hidden[s + t] = sums[t]
    for s in range(0, HALF, 4):
        updates = [
            lax.dot_general(hidden[s + t], oweight, TN, preferred_element_type=F32) for t in range(4)
        ]
        change = gate[s * LANES : (s + 4) * LANES, :] * jnp.concatenate(updates, axis=0)
        for h in range(2):
            old = [pair[s + t + h * HALF].astype(F32) for t in range(4)]
            new = [
                old[t] + change[t * LANES + h * SLOT : t * LANES + h * SLOT + SIDE] for t in range(4)
            ]
            for t in range(4):
                z_out[s + t + h * HALF] = new[t].astype(BF16)
            ready(s + h * HALF)


def middle_kernel(
    pair, gate, mixed, gain, hgain, oweight, weight, z_out, out, normed, mixed32, hidden, staged, extra
):
    finish(pair, gate, mixed, hgain[0:1, :], oweight[0], z_out, mixed32, hidden)
    normalize(z_out, gain[1:2, :], normed)
    project(normed, weight[1], staged, extra)
    write_messages(staged, out)


def last_kernel(pair, gate, mixed, hgain, oweight, z_hbm, z_out, sems, mixed32, hidden):
    copies = []

    def ready(s):
        rows = pl.ds(s, 4)
        copies.append(pltpu.make_async_copy(z_out.at[rows], z_hbm.at[rows], sems.at[s // 4]))
        copies[-1].start()

    finish(pair, gate, mixed, hgain[1:2, :], oweight[1], z_out, mixed32, hidden, ready)
    for copy in copies:
        copy.wait()


def moved(ref, p, base, offset):
    values = ref[p].astype(F32)
    lane = lane_of(EXTRA)
    tail = None
    for g in range(SIDE // PIECE):
        begin = offset + g * PIECE
        part = values[g * EXTRA : (g + 1) * EXTRA]
        shift = (begin - base - SIDE) % LANES
        part = pltpu.roll(part, shift, 1) if shift else part
        tail = part if tail is None else jnp.where((lane - begin) % LANES < PIECE, part, tail)
    shift = (offset - base) % LANES
    main = pltpu.roll(values, shift, 1) if shift else values
    return jnp.concatenate([main, tail], axis=0)


def dense(ref, which, base):
    lane = lane_of(SIDE)
    tiles = [None] * 3
    for b, p in enumerate(which):
        first, offset = divmod(b * SIDE, LANES)
        block = moved(ref, p, base, offset)
        tiles[first] = block if offset == 0 else jnp.where(lane < offset, tiles[first], block)
        if offset + SIDE > LANES:
            tiles[first + 1] = block
    return jnp.concatenate(tiles, axis=1).astype(BF16)


def split_out_kernel(got, me, left, right):
    for a in range(8):
        left[a * SIDE : (a + 1) * SIDE, :] = dense(got, [a * 8 + b for b in range(8)], 0)
    for a in range(4):
        for n, core in enumerate((me[0], 1 - me[0])):
            start = n * 192 + a * SIDE
            right[start : start + SIDE, :] = dense(got, [(2 * a + core) * 8 + b for b in range(8)], SLOT)


def send_back(total, blocks, place, out):
    lane = lane_of(HALF)
    for a in range(blocks):
        for b in range(0, 4, 2):
            tile = total[a * SIDE : (a + 1) * SIDE, b * SLOT : (b + 2) * SLOT]
            low, high = tile[:HALF], tile[HALF:]
            out[place(a, b)] = jnp.where(lane < SLOT, low, pltpu.roll(high, SLOT, 1)).astype(BF16)
            out[place(a, b + 1)] = jnp.where(lane < SLOT, pltpu.roll(low, SLOT, 1), high).astype(BF16)


def padded(ref, start):
    pad = jnp.zeros((SLOT - SIDE, ref.shape[1]), BF16)
    pieces = []
    for b in range(4):
        pieces += [ref[start + b * SIDE : start + (b + 1) * SIDE, :], pad]
    return jnp.concatenate(pieces, axis=0)


def mix_out_kernel(left, left_c, right, right_c, right_y, right_yc, me, out):
    for step, (near, far) in enumerate(((right, right_c), (right_y, right_yc))):
        total = lax.dot_general(left[...], padded(near, 0), NT, preferred_element_type=F32)
        total += lax.dot_general(left_c[...], padded(far, 192), NT, preferred_element_type=F32)
        owner = me[0] if step == 0 else 1 - me[0]
        send_back(total, 8, lambda a, b: a * 8 + (2 * (b // 2) + owner) * 2 + b % 2, out)


def split_in_kernel(got, left, right):
    for r in range(8):
        rows = slice(r * SIDE, (r + 1) * SIDE)
        left[rows, :] = dense(got, [(r + 8 * h) * 4 + b for h in range(2) for b in range(4)], 0)
    lane = lane_of(SIDE)
    for r in range(16):
        for b in range(0, 4, 2):
            low, high = moved(got, r * 4 + b, SLOT, 0), moved(got, r * 4 + b + 1, SLOT, SLOT)
            tile = jnp.where(lane < SLOT, low, high)
            right[r * SIDE : (r + 1) * SIDE, b * SLOT : (b + 2) * SLOT] = tile.astype(BF16)


def mix_in_kernel(right, left, left_c, left_x, left_d, me, out):
    for step, ref in enumerate((left, left_c, left_x, left_d)):
        tall = ref[...].T
        total = jnp.dot(tall[:192], right[:384, :], preferred_element_type=F32)
        total += jnp.dot(tall[192:], right[384:, :], preferred_element_type=F32)
        core = me[1] if step % 2 == 0 else 1 - me[1]
        low = me[0] if step < 2 else 1 - me[0]
        send_back(
            total,
            4,
            lambda a, b: (2 * (a // 2) + low) * 16 + (2 * (a % 2) + core) * 4 + b,
            out,
        )


def swap(values, *axes):
    n = 1 << len(axes)
    return lax.ppermute(values, axes, [(i, n - 1 - i) for i in range(n)])


MESSAGE = (CH, MAIN, LANES)
BACK = (CH, HALF, LANES)
BLOCK = (SIDE, SIDE, LANES)
GATE = (HALF * LANES, LANES)


def body(pair, norm_gain, proj_weight, hid_gain, out_weight, gate_weight):
    normed = pltpu.VMEM(GATE, BF16)
    staged = pltpu.VMEM((MAIN * STRIDE, LANES), F32)
    extra = pltpu.VMEM((HALF, CH, LANES), F32)
    mixed32 = pltpu.VMEM((CH * HALF, LANES), F32)
    hidden = pltpu.VMEM((HALF, CH, LANES), BF16)
    block = pltpu.VMEM(BLOCK, BF16)
    gain32, weight = pltpu.VMEM((2, LANES), F32), pltpu.VMEM((LANES, 4 * CH), BF16)
    out_axes, in_axes = ("yh", "zl", "xh", "xl", "zh"), ("yh", "yl", "zl", "xh", "zh")
    core = lax.axis_index("c")

    (sent,) = call(
        project_kernel,
        [MESSAGE],
        3,
        [block, gain32, weight, pltpu.SemaphoreType.DMA((SIDE // GROUP + 2,)), normed, staged, extra],
        inputs=HBM,
        limit=55 << 20,
    )(pair, norm_gain, proj_weight)
    (gate,) = call(functools.partial(gate_kernel, 0), [GATE], 3, [normed], dtype=F32)(pair, norm_gain, gate_weight)
    got = lax.all_to_all(sent, out_axes, 0, 0, tiled=True)
    left, right = call(split_out_kernel, [(384, 384)] * 2, 1, smem=1)(got, core.reshape(1))
    right_y = swap(right, "yl")
    (sent,) = call(mix_out_kernel, [BACK], 6, smem=1)(
        left,
        swap(left, "c"),
        right,
        swap(right, "c"),
        right_y,
        swap(right_y, "c"),
        lax.axis_index("yl").reshape(1),
    )
    mixed = lax.all_to_all(sent, out_axes, 0, 0, tiled=True)
    first, sent = call(middle_kernel, [BLOCK, MESSAGE], 7, [normed, mixed32, hidden, staged, extra])(
        pair, gate, mixed, norm_gain, hid_gain, out_weight, proj_weight
    )
    (gate,) = call(functools.partial(gate_kernel, 1), [GATE], 3, [normed], dtype=F32)(first, norm_gain, gate_weight)
    got = lax.all_to_all(sent, in_axes, 0, 0, tiled=True)
    left, right = call(split_in_kernel, [(384, 384), (768, 256)], 1)(got)
    left_x = swap(left, "xl")
    (sent,) = call(mix_in_kernel, [BACK], 5, smem=1)(
        right,
        left,
        swap(left, "c"),
        left_x,
        swap(left_x, "c"),
        jnp.stack([lax.axis_index("xl"), core]),
    )
    mixed = lax.all_to_all(sent, in_axes, 0, 0, tiled=True)
    (updated,) = call(
        last_kernel,
        [BLOCK],
        5,
        [block, pltpu.SemaphoreType.DMA((SIDE // 4,)), mixed32, hidden],
        outputs=HBM,
    )(first, gate, mixed, hid_gain, out_weight)
    return updated


def solution(mesh):
    names = ("yh", "yl", "zl", "xh", "xl", "zh", "c")
    fine = Mesh(mesh.devices.reshape(2, 2, 4, 2, 2, 2, 2), names)
    spec = P(names[:3], names[3:], None)
    return jax.shard_map(
        body,
        mesh=fine,
        in_specs=(spec, P(), P(), P(), P(), P()),
        out_specs=spec,
        check_vma=False,
    )
```

```python
import functools

import jax
import jax.numpy as jnp
from jax import lax
from jax.experimental import pallas as pl
from jax.experimental.pallas import tpu as pltpu
from jax.sharding import Mesh
from jax.sharding import PartitionSpec as P

F32, BF16 = jnp.float32, jnp.bfloat16
SIDE = 48
HALF = SIDE // 2
SLOT = 64
MAIN = 40
EXTRA = SIDE - MAIN
STRIDE = 72
GROUP = 8
PIECE = 16
CH = 64
LANES = 128
EPS = 1e-05
NT = (((1,), (1,)), ((), ()))
TN = (((0,), (0,)), ((), ()))
VMEM = pl.BlockSpec(memory_space=pltpu.VMEM)
SMEM = pl.BlockSpec(memory_space=pltpu.SMEM)
HBM = pl.BlockSpec(memory_space=pltpu.HBM)


def call(kernel, outs, n_in, scratch=(), smem=0, inputs=VMEM, outputs=VMEM, dtype=BF16, limit=16 << 20):
    return pl.pallas_call(
        kernel,
        out_shape=[jax.ShapeDtypeStruct(shape, dtype) for shape in outs],
        in_specs=[inputs] * n_in + [SMEM] * smem,
        out_specs=[outputs] * len(outs),
        scratch_shapes=scratch,
        compiler_params=pltpu.CompilerParams(vmem_limit_bytes=limit),
    )


def lane_of(rows):
    return lax.broadcasted_iota(jnp.int32, (rows, LANES), 1)


def layer_norm(values, gain, axis):
    mean = jnp.mean(values, axis=axis, keepdims=True)
    centred = values - mean
    var = jnp.mean(centred * centred, axis=axis, keepdims=True)
    return centred * lax.rsqrt(var + EPS) * gain


def sigmoid(values):
    return 0.5 * jnp.tanh(0.5 * values) + 0.5


def normalize(block, gain, normed, arrive=lambda start: None):
    pad = jnp.zeros((SLOT - SIDE, LANES), BF16)
    for start in range(0, SIDE, GROUP):
        arrive(start)
        rows = layer_norm(block[start : start + GROUP].astype(F32), gain.reshape(1, 1, LANES), 2)
        rows = rows.astype(BF16)
        for i in range(GROUP):
            base = place_of(start + i)
            normed[base : base + SIDE, :] = rows[i]
            normed[base + SIDE : base + SLOT, :] = pad


def place_of(i):
    return (i % HALF) * LANES + (i // HALF) * SLOT


def project(normed, weight, staged, extra):
    wt = weight.astype(F32).T.astype(BF16)
    lane = lane_of(CH)
    for s in ORDER:
        proj = lax.dot_general(wt, normed[s * LANES : (s + 1) * LANES, :], NT, preferred_element_type=F32)
        left = sigmoid(proj[:CH]) * proj[CH : 2 * CH]
        right = sigmoid(proj[2 * CH : 3 * CH]) * proj[3 * CH :]
        first = jnp.where(lane < SLOT, left, pltpu.roll(right, SLOT, 1))
        second = jnp.where(lane < SLOT, pltpu.roll(left, SLOT, 1), right)
        if s + HALF >= MAIN:
            for g in range(SIDE // PIECE):
                extra[g * EXTRA + s + HALF - MAIN] = pltpu.roll(second, SIDE - g * PIECE, 1)
        else:
            staged[pl.ds((s + HALF) * STRIDE, CH), :] = second
        staged[pl.ds(s * STRIDE, CH), :] = jnp.where(lane % SLOT < SIDE, first, extra[s])


ORDER = [*range(HALF - EXTRA, HALF), *range(HALF - EXTRA)]


def write_messages(staged, out):
    for channel in range(CH):
        out[channel] = staged[pl.ds(channel, MAIN, stride=STRIDE), :].astype(BF16)


def project_kernel(pair_hbm, gain_hbm, weight_hbm, out, pair, gain, weight, sems, normed, staged, extra):
    groups = SIDE // GROUP
    copies = [pltpu.make_async_copy(gain_hbm, gain, sems.at[groups])]
    for n in range(groups):
        rows = pl.ds(n * GROUP, GROUP)
        copies.append(pltpu.make_async_copy(pair_hbm.at[rows], pair.at[rows], sems.at[n]))
    copies.append(pltpu.make_async_copy(weight_hbm.at[0], weight, sems.at[groups + 1]))
    for copy in copies:
        copy.start()
    copies[0].wait()
    normalize(pair, gain[0:1, :], normed, lambda start: copies[1 + start // GROUP].wait())
    copies[-1].wait()
    project(normed, weight[...], staged, extra)
    write_messages(staged, out)


def gate_kernel(p, pair, gain, gweight, gate, normed):
    normalize(pair, gain[p : p + 1, :], normed)
    for start in range(0, HALF * LANES, 4 * LANES):
        rows = slice(start, start + 4 * LANES)
        gate[rows, :] = sigmoid(jnp.dot(normed[rows, :], gweight[p], preferred_element_type=F32))


def read_sums(mixed, mixed32):
    for channel in range(CH):
        mixed32[pl.ds(channel * HALF, HALF), :] = mixed[channel].astype(F32)


def finish(pair, gate, mixed, hgain, oweight, z_out, mixed32, hidden, ready=lambda s: None):
    hcol = hgain.T
    read_sums(mixed, mixed32)
    for s in range(0, HALF, 4):
        sums = [mixed32[pl.ds(s + t, CH, stride=HALF), :] for t in range(4)]
        sums = [layer_norm(values, hcol, 0).astype(BF16) for values in sums]
        for t in range(4):
            hidden[s + t] = sums[t]
    for s in range(0, HALF, 4):
        updates = [
            lax.dot_general(hidden[s + t], oweight, TN, preferred_element_type=F32) for t in range(4)
        ]
        change = gate[s * LANES : (s + 4) * LANES, :] * jnp.concatenate(updates, axis=0)
        for h in range(2):
            old = [pair[s + t + h * HALF].astype(F32) for t in range(4)]
            new = [
                old[t] + change[t * LANES + h * SLOT : t * LANES + h * SLOT + SIDE] for t in range(4)
            ]
            for t in range(4):
                z_out[s + t + h * HALF] = new[t].astype(BF16)
            ready(s + h * HALF)


def middle_kernel(
    pair, gate, mixed, gain, hgain, oweight, weight, z_out, out, normed, mixed32, hidden, staged, extra
):
    finish(pair, gate, mixed, hgain[0:1, :], oweight[0], z_out, mixed32, hidden)
    normalize(z_out, gain[1:2, :], normed)
    project(normed, weight[1], staged, extra)
    write_messages(staged, out)


def last_kernel(pair, gate, mixed, hgain, oweight, z_hbm, z_out, sems, mixed32, hidden):
    copies = []

    def ready(s):
        rows = pl.ds(s, 4)
        copies.append(pltpu.make_async_copy(z_out.at[rows], z_hbm.at[rows], sems.at[s // 4]))
        copies[-1].start()

    finish(pair, gate, mixed, hgain[1:2, :], oweight[1], z_out, mixed32, hidden, ready)
    for copy in copies:
        copy.wait()


def moved(ref, p, base, offset):
    values = ref[p].astype(F32)
    lane = lane_of(EXTRA)
    tail = None
    for g in range(SIDE // PIECE):
        begin = offset + g * PIECE
        part = values[g * EXTRA : (g + 1) * EXTRA]
        shift = (begin - base - SIDE) % LANES
        part = pltpu.roll(part, shift, 1) if shift else part
        tail = part if tail is None else jnp.where((lane - begin) % LANES < PIECE, part, tail)
    shift = (offset - base) % LANES
    main = pltpu.roll(values, shift, 1) if shift else values
    return jnp.concatenate([main, tail], axis=0)


def dense(ref, which, base):
    lane = lane_of(SIDE)
    tiles = [None] * 3
    for b, p in enumerate(which):
        first, offset = divmod(b * SIDE, LANES)
        block = moved(ref, p, base, offset)
        tiles[first] = block if offset == 0 else jnp.where(lane < offset, tiles[first], block)
        if offset + SIDE > LANES:
            tiles[first + 1] = block
    return jnp.concatenate(tiles, axis=1).astype(BF16)


def out_right_kernel(got, me, right):
    for a in range(4):
        for n, core in enumerate((me[0], 1 - me[0])):
            start = n * 192 + a * SIDE
            right[start : start + SIDE, :] = dense(got, [(2 * a + core) * 8 + b for b in range(8)], SLOT)


def out_left_kernel(got, left):
    for a in range(8):
        left[a * SIDE : (a + 1) * SIDE, :] = dense(got, [a * 8 + b for b in range(8)], 0)


def send_back(total, blocks, place, out):
    lane = lane_of(HALF)
    for a in range(blocks):
        for b in range(0, 4, 2):
            tile = total[a * SIDE : (a + 1) * SIDE, b * SLOT : (b + 2) * SLOT]
            low, high = tile[:HALF], tile[HALF:]
            out[place(a, b)] = jnp.where(lane < SLOT, low, pltpu.roll(high, SLOT, 1)).astype(BF16)
            out[place(a, b + 1)] = jnp.where(lane < SLOT, pltpu.roll(low, SLOT, 1), high).astype(BF16)


def padded(ref, start):
    pad = jnp.zeros((SLOT - SIDE, ref.shape[1]), BF16)
    pieces = []
    for b in range(4):
        pieces += [ref[start + b * SIDE : start + (b + 1) * SIDE, :], pad]
    return jnp.concatenate(pieces, axis=0)


def out_sums(left, left_c, near, far, place, out):
    total = lax.dot_general(left[...], padded(near, 0), NT, preferred_element_type=F32)
    total += lax.dot_general(left_c[...], padded(far, 192), NT, preferred_element_type=F32)
    send_back(total, 8, place, out)


def out_early_kernel(left, left_c, right, right_c, out):
    out_sums(left, left_c, right, right_c, lambda a, b: a * 4 + b, out)


def out_late_kernel(left, left_c, right_y, right_yc, early, me, out):
    def place(owner):
        return lambda a, b: a * 8 + (2 * (b // 2) + owner) * 2 + b % 2

    for a in range(8):
        for b in range(4):
            out[place(me[0])(a, b)] = early[a * 4 + b]
    out_sums(left, left_c, right_y, right_yc, place(1 - me[0]), out)


def in_left_kernel(got, left):
    for r in range(8):
        rows = slice(r * SIDE, (r + 1) * SIDE)
        left[rows, :] = dense(got, [(r + 8 * h) * 4 + b for h in range(2) for b in range(4)], 0)


def in_right_kernel(got, right):
    lane = lane_of(SIDE)
    for r in range(16):
        for b in range(0, 4, 2):
            low, high = moved(got, r * 4 + b, SLOT, 0), moved(got, r * 4 + b + 1, SLOT, SLOT)
            tile = jnp.where(lane < SLOT, low, high)
            right[r * SIDE : (r + 1) * SIDE, b * SLOT : (b + 2) * SLOT] = tile.astype(BF16)


def in_sums(left, right, place, out):
    tall = left[...].T
    total = jnp.dot(tall[:192], right[:384, :], preferred_element_type=F32)
    total += jnp.dot(tall[192:], right[384:, :], preferred_element_type=F32)
    send_back(total, 4, place, out)


def in_early_kernel(right, left, left_c, out):
    for n, ref in enumerate((left, left_c)):
        in_sums(ref, right, lambda a, b: n * 16 + a * 4 + b, out)


def in_late_kernel(right, left_x, left_d, early, me, core, out):
    def place(low, core):
        return lambda a, b: (2 * (a // 2) + low) * 16 + (2 * (a % 2) + core) * 4 + b

    for n, c in enumerate((core[0], 1 - core[0])):
        for a in range(4):
            for b in range(4):
                out[place(me[0], c)(a, b)] = early[n * 16 + a * 4 + b]
    in_sums(left_x, right, place(1 - me[0], core[0]), out)
    in_sums(left_d, right, place(1 - me[0], 1 - core[0]), out)


def swap(values, *axes):
    n = 1 << len(axes)
    return lax.ppermute(values, axes, [(i, n - 1 - i) for i in range(n)])


MESSAGE = (CH, MAIN, LANES)
BACK = (CH, HALF, LANES)
EARLY = (CH // 2, HALF, LANES)
BLOCK = (SIDE, SIDE, LANES)
GATE = (HALF * LANES, LANES)


def body(pair, norm_gain, proj_weight, hid_gain, out_weight, gate_weight):
    normed = pltpu.VMEM(GATE, BF16)
    staged = pltpu.VMEM((MAIN * STRIDE, LANES), F32)
    extra = pltpu.VMEM((HALF, CH, LANES), F32)
    mixed32 = pltpu.VMEM((CH * HALF, LANES), F32)
    hidden = pltpu.VMEM((HALF, CH, LANES), BF16)
    block = pltpu.VMEM(BLOCK, BF16)
    gain32, weight = pltpu.VMEM((2, LANES), F32), pltpu.VMEM((LANES, 4 * CH), BF16)
    out_axes, in_axes = ("yh", "zl", "xh", "xl", "zh"), ("yh", "yl", "zl", "xh", "zh")
    tie = lax.optimization_barrier
    pair, core, low_y, low_x = tie((pair, *(lax.axis_index(name).reshape(1) for name in ("c", "yl", "xl"))))

    (sent,) = call(
        project_kernel,
        [MESSAGE],
        3,
        [block, gain32, weight, pltpu.SemaphoreType.DMA((SIDE // GROUP + 2,)), normed, staged, extra],
        inputs=HBM,
        limit=55 << 20,
    )(pair, norm_gain, proj_weight)
    got = lax.all_to_all(sent, out_axes, 0, 0, tiled=True)
    (right,) = call(out_right_kernel, [(384, 384)], 1, smem=1)(got, core)
    right_y, right_c = swap(right, "yl"), swap(right, "c")
    got, right = tie((got, right))
    (left,) = call(out_left_kernel, [(384, 384)], 1)(got)
    left_c = swap(left, "c")
    source, left = tie((pair, left))
    (gate,) = call(functools.partial(gate_kernel, 0), [GATE], 3, [normed], dtype=F32)(source, norm_gain, gate_weight)
    (early,) = call(out_early_kernel, [EARLY], 4)(left, left_c, right, right_c)
    right_y, early, gate = tie((right_y, early, gate))
    right_yc = swap(right_y, "c")
    (sent,) = call(out_late_kernel, [BACK], 5, smem=1)(left, left_c, right_y, right_yc, early, low_y)
    mixed = lax.all_to_all(sent, out_axes, 0, 0, tiled=True)
    first, sent = call(middle_kernel, [BLOCK, MESSAGE], 7, [normed, mixed32, hidden, staged, extra])(
        pair, gate, mixed, norm_gain, hid_gain, out_weight, proj_weight
    )
    got = lax.all_to_all(sent, in_axes, 0, 0, tiled=True)
    (left,) = call(in_left_kernel, [(384, 384)], 1)(got)
    left_x, left_c = swap(left, "xl"), swap(left, "c")
    got, left = tie((got, left))
    (right,) = call(in_right_kernel, [(768, 256)], 1)(got)
    source, right = tie((first, right))
    (gate,) = call(functools.partial(gate_kernel, 1), [GATE], 3, [normed], dtype=F32)(source, norm_gain, gate_weight)
    (early,) = call(in_early_kernel, [EARLY], 3)(right, left, left_c)
    left_x, early, gate = tie((left_x, early, gate))
    left_d = swap(left_x, "c")
    (sent,) = call(in_late_kernel, [BACK], 4, smem=2)(right, left_x, left_d, early, low_x, core)
    mixed = lax.all_to_all(sent, in_axes, 0, 0, tiled=True)
    (updated,) = call(
        last_kernel,
        [BLOCK],
        5,
        [block, pltpu.SemaphoreType.DMA((SIDE // 4,)), mixed32, hidden],
        outputs=HBM,
    )(first, gate, mixed, hid_gain, out_weight)
    return updated


def solution(mesh):
    names = ("yh", "yl", "zl", "xh", "xl", "zh", "c")
    fine = Mesh(mesh.devices.reshape(2, 2, 4, 2, 2, 2, 2), names)
    spec = P(names[:3], names[3:], None)
    return jax.shard_map(
        body,
        mesh=fine,
        in_specs=(spec, P(), P(), P(), P(), P()),
        out_specs=spec,
        check_vma=False,
    )
```

```python
import functools

import jax
import jax.numpy as jnp
from jax import lax
from jax.experimental import pallas as pl
from jax.experimental.pallas import tpu as pltpu
from jax.sharding import Mesh
from jax.sharding import PartitionSpec as P

F32, BF16 = jnp.float32, jnp.bfloat16
SIDE = 48
HALF = SIDE // 2
SLOT = 64
MAIN = 40
EXTRA = SIDE - MAIN
STRIDE = 72
GROUP = 8
PIECE = 16
CH = 64
LANES = 128
EPS = 1e-05
NT = (((1,), (1,)), ((), ()))
TN = (((0,), (0,)), ((), ()))
VMEM = pl.BlockSpec(memory_space=pltpu.VMEM)
SMEM = pl.BlockSpec(memory_space=pltpu.SMEM)
HBM = pl.BlockSpec(memory_space=pltpu.HBM)


def call(kernel, outs, n_in, scratch=(), smem=0, inputs=VMEM, outputs=VMEM, dtype=BF16, limit=16 << 20):
    return pl.pallas_call(
        kernel,
        out_shape=[jax.ShapeDtypeStruct(shape, dtype) for shape in outs],
        in_specs=[inputs] * n_in + [SMEM] * smem,
        out_specs=[outputs] * len(outs),
        scratch_shapes=scratch,
        compiler_params=pltpu.CompilerParams(vmem_limit_bytes=limit),
    )


def lane_of(rows):
    return lax.broadcasted_iota(jnp.int32, (rows, LANES), 1)


def layer_norm(values, gain, axis):
    mean = jnp.mean(values, axis=axis, keepdims=True)
    centred = values - mean
    var = jnp.mean(centred * centred, axis=axis, keepdims=True)
    return centred * lax.rsqrt(var + EPS) * gain


def sigmoid(values):
    return 0.5 * jnp.tanh(0.5 * values) + 0.5


def normalize(block, gain, normed, arrive=lambda start: None):
    pad = jnp.zeros((SLOT - SIDE, LANES), BF16)
    for start in range(0, SIDE, GROUP):
        arrive(start)
        rows = layer_norm(block[start : start + GROUP].astype(F32), gain.reshape(1, 1, LANES), 2)
        rows = rows.astype(BF16)
        for i in range(GROUP):
            base = place_of(start + i)
            normed[base : base + SIDE, :] = rows[i]
            normed[base + SIDE : base + SLOT, :] = pad


def place_of(i):
    return (i % HALF) * LANES + (i // HALF) * SLOT


def project(normed, weight, staged, extra):
    wt = weight.astype(F32).T.astype(BF16)
    lane = lane_of(CH)
    for s in ORDER:
        proj = lax.dot_general(wt, normed[s * LANES : (s + 1) * LANES, :], NT, preferred_element_type=F32)
        left = sigmoid(proj[:CH]) * proj[CH : 2 * CH]
        right = sigmoid(proj[2 * CH : 3 * CH]) * proj[3 * CH :]
        first = jnp.where(lane < SLOT, left, pltpu.roll(right, SLOT, 1))
        second = jnp.where(lane < SLOT, pltpu.roll(left, SLOT, 1), right)
        if s + HALF >= MAIN:
            for g in range(SIDE // PIECE):
                extra[g * EXTRA + s + HALF - MAIN] = pltpu.roll(second, SIDE - g * PIECE, 1)
        else:
            staged[pl.ds((s + HALF) * STRIDE, CH), :] = second
        staged[pl.ds(s * STRIDE, CH), :] = jnp.where(lane % SLOT < SIDE, first, extra[s])


ORDER = [*range(HALF - EXTRA, HALF), *range(HALF - EXTRA)]


def write_messages(staged, out):
    for channel in range(CH):
        out[channel] = staged[pl.ds(channel, MAIN, stride=STRIDE), :].astype(BF16)


def project_kernel(pair_hbm, gain_hbm, weight_hbm, out, pair, gain, weight, sems, normed, staged, extra):
    groups = SIDE // GROUP
    copies = [pltpu.make_async_copy(gain_hbm, gain, sems.at[groups])]
    for n in range(groups):
        rows = pl.ds(n * GROUP, GROUP)
        copies.append(pltpu.make_async_copy(pair_hbm.at[rows], pair.at[rows], sems.at[n]))
    copies.append(pltpu.make_async_copy(weight_hbm.at[0], weight, sems.at[groups + 1]))
    for copy in copies:
        copy.start()
    copies[0].wait()
    normalize(pair, gain[0:1, :], normed, lambda start: copies[1 + start // GROUP].wait())
    copies[-1].wait()
    project(normed, weight[...], staged, extra)
    write_messages(staged, out)


def gate_kernel(p, pair, gain, gweight, gate, normed):
    normalize(pair, gain[p : p + 1, :], normed)
    for start in range(0, HALF * LANES, 4 * LANES):
        rows = slice(start, start + 4 * LANES)
        gate[rows, :] = sigmoid(jnp.dot(normed[rows, :], gweight[p], preferred_element_type=F32))


def read_sums(mixed, mixed32):
    for channel in range(CH):
        mixed32[pl.ds(channel * HALF, HALF), :] = mixed[channel].astype(F32)


def finish(pair, gate, mixed, hgain, oweight, z_out, mixed32, hidden, ready=lambda s: None):
    hcol = hgain.T
    read_sums(mixed, mixed32)
    for s in range(0, HALF, 4):
        sums = [mixed32[pl.ds(s + t, CH, stride=HALF), :] for t in range(4)]
        sums = [layer_norm(values, hcol, 0).astype(BF16) for values in sums]
        for t in range(4):
            hidden[s + t] = sums[t]
    for s in range(0, HALF, 4):
        updates = [
            lax.dot_general(hidden[s + t], oweight, TN, preferred_element_type=F32) for t in range(4)
        ]
        change = gate[s * LANES : (s + 4) * LANES, :] * jnp.concatenate(updates, axis=0)
        for h in range(2):
            old = [pair[s + t + h * HALF].astype(F32) for t in range(4)]
            new = [
                old[t] + change[t * LANES + h * SLOT : t * LANES + h * SLOT + SIDE] for t in range(4)
            ]
            for t in range(4):
                z_out[s + t + h * HALF] = new[t].astype(BF16)
            ready(s + h * HALF)


def middle_kernel(
    pair, gate, mixed, gain, hgain, oweight, weight, z_out, out, normed, mixed32, hidden, staged, extra
):
    finish(pair, gate, mixed, hgain[0:1, :], oweight[0], z_out, mixed32, hidden)
    normalize(z_out, gain[1:2, :], normed)
    project(normed, weight[1], staged, extra)
    write_messages(staged, out)


def last_kernel(pair, gate, mixed, hgain, oweight, z_hbm, z_out, sems, mixed32, hidden):
    copies = []

    def ready(s):
        rows = pl.ds(s, 4)
        copies.append(pltpu.make_async_copy(z_out.at[rows], z_hbm.at[rows], sems.at[s // 4]))
        copies[-1].start()

    finish(pair, gate, mixed, hgain[1:2, :], oweight[1], z_out, mixed32, hidden, ready)
    for copy in copies:
        copy.wait()


def moved(ref, p, base, offset):
    values = ref[p].astype(F32)
    lane = lane_of(EXTRA)
    tail = None
    for g in range(SIDE // PIECE):
        begin = offset + g * PIECE
        part = values[g * EXTRA : (g + 1) * EXTRA]
        shift = (begin - base - SIDE) % LANES
        part = pltpu.roll(part, shift, 1) if shift else part
        tail = part if tail is None else jnp.where((lane - begin) % LANES < PIECE, part, tail)
    shift = (offset - base) % LANES
    main = pltpu.roll(values, shift, 1) if shift else values
    return jnp.concatenate([main, tail], axis=0)


def dense(ref, which, base):
    lane = lane_of(SIDE)
    tiles = [None] * 3
    for b, p in enumerate(which):
        first, offset = divmod(b * SIDE, LANES)
        block = moved(ref, p, base, offset)
        tiles[first] = block if offset == 0 else jnp.where(lane < offset, tiles[first], block)
        if offset + SIDE > LANES:
            tiles[first + 1] = block
    return jnp.concatenate(tiles, axis=1).astype(BF16)


def out_right_kernel(got, me, right):
    for a in range(4):
        for n, core in enumerate((me[0], 1 - me[0])):
            start = n * 192 + a * SIDE
            right[start : start + SIDE, :] = dense(got, [(2 * a + core) * 8 + b for b in range(8)], SLOT)


def out_left_kernel(got, left):
    for a in range(8):
        left[a * SIDE : (a + 1) * SIDE, :] = dense(got, [a * 8 + b for b in range(8)], 0)


def send_back(total, blocks, place, out):
    lane = lane_of(HALF)
    for a in range(blocks):
        for b in range(0, 4, 2):
            tile = total[a * SIDE : (a + 1) * SIDE, b * SLOT : (b + 2) * SLOT]
            low, high = tile[:HALF], tile[HALF:]
            out[place(a, b)] = jnp.where(lane < SLOT, low, pltpu.roll(high, SLOT, 1)).astype(BF16)
            out[place(a, b + 1)] = jnp.where(lane < SLOT, pltpu.roll(low, SLOT, 1), high).astype(BF16)


def padded(ref, start):
    pad = jnp.zeros((SLOT - SIDE, ref.shape[1]), BF16)
    pieces = []
    for b in range(4):
        pieces += [ref[start + b * SIDE : start + (b + 1) * SIDE, :], pad]
    return jnp.concatenate(pieces, axis=0)


def mix_out_kernel(left, left_c, right, right_c, right_y, right_yc, me, out):
    for step, (near, far) in enumerate(((right, right_c), (right_y, right_yc))):
        total = lax.dot_general(left[...], padded(near, 0), NT, preferred_element_type=F32)
        total += lax.dot_general(left_c[...], padded(far, 192), NT, preferred_element_type=F32)
        owner = me[0] if step == 0 else 1 - me[0]
        send_back(total, 8, lambda a, b: a * 8 + (2 * (b // 2) + owner) * 2 + b % 2, out)


def in_left_kernel(got, out, left):
    for r in range(8):
        rows = slice(r * SIDE, (r + 1) * SIDE)
        left[rows, :] = dense(got, [(r + 8 * h) * 4 + b for h in range(2) for b in range(4)], 0)
    out[...] = left[...].T


def in_right_kernel(got, right):
    lane = lane_of(SIDE)
    for r in range(16):
        for b in range(0, 4, 2):
            low, high = moved(got, r * 4 + b, SLOT, 0), moved(got, r * 4 + b + 1, SLOT, SLOT)
            tile = jnp.where(lane < SLOT, low, high)
            right[r * SIDE : (r + 1) * SIDE, b * SLOT : (b + 2) * SLOT] = tile.astype(BF16)


def mix_in_kernel(right, left, left_c, left_x, left_d, me, core, out):
    for step, ref in enumerate((left, left_c, left_x, left_d)):
        total = jnp.dot(ref[:192, :], right[:384, :], preferred_element_type=F32)
        total += jnp.dot(ref[192:, :], right[384:, :], preferred_element_type=F32)
        c = core[0] if step % 2 == 0 else 1 - core[0]
        low = me[0] if step < 2 else 1 - me[0]
        send_back(
            total,
            4,
            lambda a, b: (2 * (a // 2) + low) * 16 + (2 * (a % 2) + c) * 4 + b,
            out,
        )


def swap(values, *axes):
    n = 1 << len(axes)
    return lax.ppermute(values, axes, [(i, n - 1 - i) for i in range(n)])


MESSAGE = (CH, MAIN, LANES)
BACK = (CH, HALF, LANES)
BLOCK = (SIDE, SIDE, LANES)
GATE = (HALF * LANES, LANES)


def body(pair, norm_gain, proj_weight, hid_gain, out_weight, gate_weight):
    normed = pltpu.VMEM(GATE, BF16)
    staged = pltpu.VMEM((MAIN * STRIDE, LANES), F32)
    extra = pltpu.VMEM((HALF, CH, LANES), F32)
    mixed32 = pltpu.VMEM((CH * HALF, LANES), F32)
    hidden = pltpu.VMEM((HALF, CH, LANES), BF16)
    block = pltpu.VMEM(BLOCK, BF16)
    gain32, weight = pltpu.VMEM((2, LANES), F32), pltpu.VMEM((LANES, 4 * CH), BF16)
    out_axes, in_axes = ("yh", "zl", "xh", "xl", "zh"), ("yh", "yl", "zl", "xh", "zh")
    tie = lax.optimization_barrier
    pair, core, low_y, low_x = tie((pair, *(lax.axis_index(name).reshape(1) for name in ("c", "yl", "xl"))))

    (sent,) = call(
        project_kernel,
        [MESSAGE],
        3,
        [block, gain32, weight, pltpu.SemaphoreType.DMA((SIDE // GROUP + 2,)), normed, staged, extra],
        inputs=HBM,
        limit=55 << 20,
    )(pair, norm_gain, proj_weight)
    got = lax.all_to_all(sent, out_axes, 0, 0, tiled=True)
    (right,) = call(out_right_kernel, [(384, 384)], 1, smem=1)(got, core)
    right_y, right_c = swap(right, "yl"), swap(right, "c")
    got, right = tie((got, right))
    (left,) = call(out_left_kernel, [(384, 384)], 1)(got)
    left_c = swap(left, "c")
    source, left = tie((pair, left))
    (gate,) = call(functools.partial(gate_kernel, 0), [GATE], 3, [normed], dtype=F32)(source, norm_gain, gate_weight)
    right_y, gate = tie((right_y, gate))
    (sent,) = call(mix_out_kernel, [BACK], 6, smem=1)(
        left, left_c, right, right_c, right_y, swap(right_y, "c"), low_y
    )
    mixed = lax.all_to_all(sent, out_axes, 0, 0, tiled=True)
    first, sent = call(middle_kernel, [BLOCK, MESSAGE], 7, [normed, mixed32, hidden, staged, extra])(
        pair, gate, mixed, norm_gain, hid_gain, out_weight, proj_weight
    )
    got = lax.all_to_all(sent, in_axes, 0, 0, tiled=True)
    (left,) = call(in_left_kernel, [(384, 384)], 1, [pltpu.VMEM((384, 384), BF16)])(got)
    left_x, left_c = swap(left, "xl"), swap(left, "c")
    got, left = tie((got, left))
    (right,) = call(in_right_kernel, [(768, 256)], 1)(got)
    source, right = tie((first, right))
    (gate,) = call(functools.partial(gate_kernel, 1), [GATE], 3, [normed], dtype=F32)(source, norm_gain, gate_weight)
    left_x, gate = tie((left_x, gate))
    (sent,) = call(mix_in_kernel, [BACK], 5, smem=2)(right, left, left_c, left_x, swap(left_x, "c"), low_x, core)
    mixed = lax.all_to_all(sent, in_axes, 0, 0, tiled=True)
    (updated,) = call(
        last_kernel,
        [BLOCK],
        5,
        [block, pltpu.SemaphoreType.DMA((SIDE // 4,)), mixed32, hidden],
        outputs=HBM,
    )(first, gate, mixed, hid_gain, out_weight)
    return updated


def solution(mesh):
    names = ("yh", "yl", "zl", "xh", "xl", "zh", "c")
    fine = Mesh(mesh.devices.reshape(2, 2, 4, 2, 2, 2, 2), names)
    spec = P(names[:3], names[3:], None)
    return jax.shard_map(
        body,
        mesh=fine,
        in_specs=(spec, P(), P(), P(), P(), P()),
        out_specs=spec,
        check_vma=False,
    )
```

```python
import functools

import jax
import jax.numpy as jnp
from jax import lax
from jax.experimental import pallas as pl
from jax.experimental.pallas import tpu as pltpu
from jax.sharding import Mesh
from jax.sharding import PartitionSpec as P

F32, BF16 = jnp.float32, jnp.bfloat16
SIDE = 48
HALF = SIDE // 2
SLOT = 64
MAIN = 40
EXTRA = SIDE - MAIN
STRIDE = 72
GROUP = 16
KEPT = 18
PIECE = 16
CH = 64
LANES = 128
EPS = 1e-05
NT = (((1,), (1,)), ((), ()))
TN = (((0,), (0,)), ((), ()))
VMEM = pl.BlockSpec(memory_space=pltpu.VMEM)
SMEM = pl.BlockSpec(memory_space=pltpu.SMEM)
HBM = pl.BlockSpec(memory_space=pltpu.HBM)


def call(kernel, outs, n_in, scratch=(), smem=0, inputs=VMEM, outputs=VMEM, dtype=BF16, limit=16 << 20):
    return pl.pallas_call(
        kernel,
        out_shape=[jax.ShapeDtypeStruct(shape, dtype) for shape in outs],
        in_specs=[inputs] * n_in + [SMEM] * smem,
        out_specs=[outputs] * len(outs),
        scratch_shapes=scratch,
        compiler_params=pltpu.CompilerParams(vmem_limit_bytes=limit),
    )


def lane_of(rows):
    return lax.broadcasted_iota(jnp.int32, (rows, LANES), 1)


def layer_norm(values, gain, axis):
    mean = jnp.mean(values, axis=axis, keepdims=True)
    centred = values - mean
    var = jnp.mean(centred * centred, axis=axis, keepdims=True)
    return centred * lax.rsqrt(var + EPS) * gain


def sigmoid(values):
    return 0.5 * jnp.tanh(0.5 * values) + 0.5


def normalize(block, gain, normed, arrive=lambda start: None):
    pad = jnp.zeros((SLOT - SIDE, LANES), BF16)
    for start in range(0, SIDE, GROUP):
        arrive(start)
        rows = layer_norm(block[start : start + GROUP].astype(F32), gain.reshape(1, 1, LANES), 2)
        rows = rows.astype(BF16)
        for i in range(GROUP):
            base = place_of(start + i)
            normed[base : base + SIDE, :] = rows[i]
            normed[base + SIDE : base + SLOT, :] = pad


def place_of(i):
    return (i % HALF) * LANES + (i // HALF) * SLOT


def project(normed, weight, staged, extra):
    wt = weight.astype(F32).T.astype(BF16)
    lane = lane_of(CH)
    for s in ORDER:
        proj = lax.dot_general(wt, normed[s * LANES : (s + 1) * LANES, :], NT, preferred_element_type=F32)
        left = sigmoid(proj[:CH]) * proj[CH : 2 * CH]
        right = sigmoid(proj[2 * CH : 3 * CH]) * proj[3 * CH :]
        first = jnp.where(lane < SLOT, left, pltpu.roll(right, SLOT, 1))
        second = jnp.where(lane < SLOT, pltpu.roll(left, SLOT, 1), right)
        if s + HALF >= MAIN:
            for g in range(SIDE // PIECE):
                extra[g * EXTRA + s + HALF - MAIN] = pltpu.roll(second, SIDE - g * PIECE, 1)
        else:
            staged[pl.ds((s + HALF) * STRIDE, CH), :] = second
        staged[pl.ds(s * STRIDE, CH), :] = jnp.where(lane % SLOT < SIDE, first, extra[s])


ORDER = [*range(HALF - EXTRA, HALF), *range(HALF - EXTRA)]


def write_messages(staged, out):
    for channel in range(CH):
        out[channel] = staged[pl.ds(channel, MAIN, stride=STRIDE), :].astype(BF16)


def project_kernel(pair_hbm, gain_hbm, weight_hbm, out, pair, gain, weight, sems, normed, staged, extra):
    groups = SIDE // GROUP
    copies = [pltpu.make_async_copy(gain_hbm, gain, sems.at[groups])]
    for n in range(groups):
        rows = pl.ds(n * GROUP, GROUP)
        copies.append(pltpu.make_async_copy(pair_hbm.at[rows], pair.at[rows], sems.at[n]))
    copies.append(pltpu.make_async_copy(weight_hbm.at[0], weight, sems.at[groups + 1]))
    for copy in copies:
        copy.start()
    copies[0].wait()
    normalize(pair, gain[0:1, :], normed, lambda start: copies[1 + start // GROUP].wait())
    copies[-1].wait()
    project(normed, weight[...], staged, extra)
    write_messages(staged, out)


def gate_kernel(p, pair, gain, gweight, gate, normed):
    normalize(pair, gain[p : p + 1, :], normed)
    for start in range(0, HALF * LANES, 4 * LANES):
        rows = slice(start, start + 4 * LANES)
        gate[rows, :] = sigmoid(jnp.dot(normed[rows, :], gweight[p], preferred_element_type=F32))


def read_sums(mixed, mixed32):
    for channel in range(CH):
        for t in range(KEPT // 2):
            tile = mixed[channel, :, t * LANES : (t + 1) * LANES].astype(F32)
            mixed32[pl.ds(channel * HALF + 2 * t, 2), :] = tile


def sums_of(mixed32, s):
    if s < KEPT:
        return mixed32[pl.ds(s, CH, stride=HALF), :]
    lane, sums = lane_of(CH) % SLOT, None
    for g in range(SIDE // PIECE):
        part = mixed32[pl.ds(g * (HALF - KEPT) + s - KEPT, CH, stride=HALF), :]
        part = pltpu.roll(part, LANES - SIDE + g * PIECE, 1)
        sums = part if sums is None else jnp.where(lane < g * PIECE, sums, part)
    return sums


def finish(pair, gate, mixed, hgain, oweight, z_out, mixed32, hidden, ready=lambda s: None):
    hcol = hgain.T
    read_sums(mixed, mixed32)
    for s in range(0, HALF, 4):
        sums = [sums_of(mixed32, s + t) for t in range(4)]
        sums = [layer_norm(values, hcol, 0).astype(BF16) for values in sums]
        for t in range(4):
            hidden[s + t] = sums[t]
    for s in range(0, HALF, 4):
        updates = [
            lax.dot_general(hidden[s + t], oweight, TN, preferred_element_type=F32) for t in range(4)
        ]
        change = gate[s * LANES : (s + 4) * LANES, :] * jnp.concatenate(updates, axis=0)
        for h in range(2):
            old = [pair[s + t + h * HALF].astype(F32) for t in range(4)]
            new = [
                old[t] + change[t * LANES + h * SLOT : t * LANES + h * SLOT + SIDE] for t in range(4)
            ]
            for t in range(4):
                z_out[s + t + h * HALF] = new[t].astype(BF16)
            ready(s + h * HALF)


def middle_kernel(
    pair, gate, mixed, gain, hgain, oweight, weight, z_out, out, normed, mixed32, hidden, staged, extra
):
    finish(pair, gate, mixed, hgain[0:1, :], oweight[0], z_out, mixed32, hidden)
    normalize(z_out, gain[1:2, :], normed)
    project(normed, weight[1], staged, extra)
    write_messages(staged, out)


def last_kernel(pair, gate, mixed, hgain, oweight, z_hbm, z_out, sems, mixed32, hidden):
    copies = []

    def ready(s):
        rows = pl.ds(s, 4)
        copies.append(pltpu.make_async_copy(z_out.at[rows], z_hbm.at[rows], sems.at[s // 4]))
        copies[-1].start()

    finish(pair, gate, mixed, hgain[1:2, :], oweight[1], z_out, mixed32, hidden, ready)
    for copy in copies:
        copy.wait()


def moved(ref, p, base, offset):
    values = ref[p].astype(F32)
    lane = lane_of(EXTRA)
    tail = None
    for g in range(SIDE // PIECE):
        begin = offset + g * PIECE
        part = values[g * EXTRA : (g + 1) * EXTRA]
        shift = (begin - base - SIDE) % LANES
        part = pltpu.roll(part, shift, 1) if shift else part
        tail = part if tail is None else jnp.where((lane - begin) % LANES < PIECE, part, tail)
    shift = (offset - base) % LANES
    main = pltpu.roll(values, shift, 1) if shift else values
    return jnp.concatenate([main, tail], axis=0)


def dense(ref, which, base):
    lane = lane_of(SIDE)
    tiles = [None] * 3
    for b, p in enumerate(which):
        first, offset = divmod(b * SIDE, LANES)
        block = moved(ref, p, base, offset)
        tiles[first] = block if offset == 0 else jnp.where(lane < offset, tiles[first], block)
        if offset + SIDE > LANES:
            tiles[first + 1] = block
    return jnp.concatenate(tiles, axis=1).astype(BF16)


def out_right_kernel(got, me, right):
    for a in range(4):
        for n, core in enumerate((me[0], 1 - me[0])):
            start = n * 192 + a * SIDE
            right[start : start + SIDE, :] = dense(got, [(2 * a + core) * 8 + b for b in range(8)], SLOT)


def out_left_kernel(got, left):
    for a in range(8):
        left[a * SIDE : (a + 1) * SIDE, :] = dense(got, [a * 8 + b for b in range(8)], 0)


def send_back(total, blocks, place, out):
    lane = lane_of(HALF)
    for a in range(blocks):
        for b in range(0, 4, 2):
            tile = total[a * SIDE : (a + 1) * SIDE, b * SLOT : (b + 2) * SLOT]
            low, high = tile[:HALF], tile[HALF:]
            write_sums(jnp.where(lane < SLOT, low, pltpu.roll(high, SLOT, 1)), place(a, b), out)
            write_sums(jnp.where(lane < SLOT, pltpu.roll(low, SLOT, 1), high), place(a, b + 1), out)


def write_sums(rows, p, out):
    last = rows[16:]
    spare = [pltpu.roll(last, SIDE - g * PIECE, 1)[KEPT - 16 :] for g in range(SIDE // PIECE)]
    lane = lane_of(KEPT) % SLOT
    rows = jnp.where(lane < SIDE, rows[:KEPT], jnp.concatenate(spare, axis=0)).astype(BF16)
    for t in range(KEPT // 2):
        out[p, :, t * LANES : (t + 1) * LANES] = rows[2 * t : 2 * t + 2]


def padded(ref, start):
    pad = jnp.zeros((SLOT - SIDE, ref.shape[1]), BF16)
    pieces = []
    for b in range(4):
        pieces += [ref[start + b * SIDE : start + (b + 1) * SIDE, :], pad]
    return jnp.concatenate(pieces, axis=0)


def mix_out_kernel(left, left_c, right, right_c, right_y, right_yc, me, out):
    for step, (near, far) in enumerate(((right, right_c), (right_y, right_yc))):
        total = lax.dot_general(left[...], padded(near, 0), NT, preferred_element_type=F32)
        total += lax.dot_general(left_c[...], padded(far, 192), NT, preferred_element_type=F32)
        owner = me[0] if step == 0 else 1 - me[0]
        send_back(total, 8, lambda a, b: a * 8 + (2 * (b // 2) + owner) * 2 + b % 2, out)


def in_left_kernel(got, out, left):
    for r in range(8):
        rows = slice(r * SIDE, (r + 1) * SIDE)
        left[rows, :] = dense(got, [(r + 8 * h) * 4 + b for h in range(2) for b in range(4)], 0)
    out[...] = left[...].T


def in_right_kernel(got, right):
    lane = lane_of(SIDE)
    for r in range(16):
        for b in range(0, 4, 2):
            low, high = moved(got, r * 4 + b, SLOT, 0), moved(got, r * 4 + b + 1, SLOT, SLOT)
            tile = jnp.where(lane < SLOT, low, high)
            right[r * SIDE : (r + 1) * SIDE, b * SLOT : (b + 2) * SLOT] = tile.astype(BF16)


def mix_in_kernel(right, left, left_c, left_x, left_d, me, core, out):
    for step, ref in enumerate((left, left_c, left_x, left_d)):
        total = jnp.dot(ref[:192, :], right[:384, :], preferred_element_type=F32)
        total += jnp.dot(ref[192:, :], right[384:, :], preferred_element_type=F32)
        c = core[0] if step % 2 == 0 else 1 - core[0]
        low = me[0] if step < 2 else 1 - me[0]
        send_back(
            total,
            4,
            lambda a, b: (2 * (a // 2) + low) * 16 + (2 * (a % 2) + c) * 4 + b,
            out,
        )


def swap(values, *axes):
    n = 1 << len(axes)
    return lax.ppermute(values, axes, [(i, n - 1 - i) for i in range(n)])


MESSAGE = (CH, MAIN, LANES)
BACK = (CH, 2, KEPT // 2 * LANES)
BLOCK = (SIDE, SIDE, LANES)
GATE = (HALF * LANES, LANES)


def body(pair, norm_gain, proj_weight, hid_gain, out_weight, gate_weight):
    normed = pltpu.VMEM(GATE, BF16)
    staged = pltpu.VMEM((MAIN * STRIDE, LANES), F32)
    extra = pltpu.VMEM((HALF, CH, LANES), F32)
    mixed32 = pltpu.VMEM((CH * HALF, LANES), F32)
    hidden = pltpu.VMEM((HALF, CH, LANES), BF16)
    block = pltpu.VMEM(BLOCK, BF16)
    gain32, weight = pltpu.VMEM((2, LANES), F32), pltpu.VMEM((LANES, 4 * CH), BF16)
    out_axes, in_axes = ("yh", "zl", "xh", "xl", "zh"), ("yh", "yl", "zl", "xh", "zh")
    tie = lax.optimization_barrier
    pair, core, low_y, low_x = tie((pair, *(lax.axis_index(name).reshape(1) for name in ("c", "yl", "xl"))))

    (sent,) = call(
        project_kernel,
        [MESSAGE],
        3,
        [block, gain32, weight, pltpu.SemaphoreType.DMA((SIDE // GROUP + 2,)), normed, staged, extra],
        inputs=HBM,
        limit=55 << 20,
    )(pair, norm_gain, proj_weight)
    got = lax.all_to_all(sent, out_axes, 0, 0, tiled=True)
    (right,) = call(out_right_kernel, [(384, 384)], 1, smem=1)(got, core)
    right_y, right_c = swap(right, "yl"), swap(right, "c")
    got, right = tie((got, right))
    (left,) = call(out_left_kernel, [(384, 384)], 1)(got)
    left_c = swap(left, "c")
    source, left = tie((pair, left))
    (gate,) = call(functools.partial(gate_kernel, 0), [GATE], 3, [normed], dtype=F32)(source, norm_gain, gate_weight)
    right_y, gate = tie((right_y, gate))
    (sent,) = call(mix_out_kernel, [BACK], 6, smem=1)(
        left, left_c, right, right_c, right_y, swap(right_y, "c"), low_y
    )
    mixed = lax.all_to_all(sent, out_axes, 0, 0, tiled=True)
    first, sent = call(middle_kernel, [BLOCK, MESSAGE], 7, [normed, mixed32, hidden, staged, extra])(
        pair, gate, mixed, norm_gain, hid_gain, out_weight, proj_weight
    )
    got = lax.all_to_all(sent, in_axes, 0, 0, tiled=True)
    (left,) = call(in_left_kernel, [(384, 384)], 1, [pltpu.VMEM((384, 384), BF16)])(got)
    left_x, left_c = swap(left, "xl"), swap(left, "c")
    got, left = tie((got, left))
    (right,) = call(in_right_kernel, [(768, 256)], 1)(got)
    source, right = tie((first, right))
    (gate,) = call(functools.partial(gate_kernel, 1), [GATE], 3, [normed], dtype=F32)(source, norm_gain, gate_weight)
    left_x, gate = tie((left_x, gate))
    (sent,) = call(mix_in_kernel, [BACK], 5, smem=2)(right, left, left_c, left_x, swap(left_x, "c"), low_x, core)
    mixed = lax.all_to_all(sent, in_axes, 0, 0, tiled=True)
    (updated,) = call(
        last_kernel,
        [BLOCK],
        5,
        [block, pltpu.SemaphoreType.DMA((SIDE // 4,)), mixed32, hidden],
        outputs=HBM,
    )(first, gate, mixed, hid_gain, out_weight)
    return updated


def solution(mesh):
    names = ("yh", "yl", "zl", "xh", "xl", "zh", "c")
    fine = Mesh(mesh.devices.reshape(2, 2, 4, 2, 2, 2, 2), names)
    spec = P(names[:3], names[3:], None)
    return jax.shard_map(
        body,
        mesh=fine,
        in_specs=(spec, P(), P(), P(), P(), P()),
        out_specs=spec,
        check_vma=False,
    )
```

```python
import functools

import jax
import jax.numpy as jnp
from jax import lax
from jax.experimental import pallas as pl
from jax.experimental.pallas import tpu as pltpu
from jax.sharding import Mesh
from jax.sharding import PartitionSpec as P

F32, BF16 = jnp.float32, jnp.bfloat16
SIDE = 48
HALF = SIDE // 2
SLOT = 64
MAIN = 36
TILE = 4
TILES = MAIN // TILE
EXTRA = SIDE - MAIN
STRIDE = 72
GROUP = 16
KEPT = 18
PIECE = 16
CH = 64
LANES = 128
EPS = 1e-05
NT = (((1,), (1,)), ((), ()))
TN = (((0,), (0,)), ((), ()))
VMEM = pl.BlockSpec(memory_space=pltpu.VMEM)
SMEM = pl.BlockSpec(memory_space=pltpu.SMEM)
HBM = pl.BlockSpec(memory_space=pltpu.HBM)


def call(kernel, outs, n_in, scratch=(), smem=0, inputs=VMEM, outputs=VMEM, dtype=BF16, limit=16 << 20):
    return pl.pallas_call(
        kernel,
        out_shape=[jax.ShapeDtypeStruct(shape, dtype) for shape in outs],
        in_specs=[inputs] * n_in + [SMEM] * smem,
        out_specs=[outputs] * len(outs),
        scratch_shapes=scratch,
        compiler_params=pltpu.CompilerParams(vmem_limit_bytes=limit),
    )


def lane_of(rows):
    return lax.broadcasted_iota(jnp.int32, (rows, LANES), 1)


def layer_norm(values, gain, axis):
    mean = jnp.mean(values, axis=axis, keepdims=True)
    centred = values - mean
    var = jnp.mean(centred * centred, axis=axis, keepdims=True)
    return centred * lax.rsqrt(var + EPS) * gain


def sigmoid(values):
    return 0.5 * jnp.tanh(0.5 * values) + 0.5


def normalize(block, gain, normed, arrive=lambda start: None):
    pad = jnp.zeros((SLOT - SIDE, LANES), BF16)
    for start in range(0, SIDE, GROUP):
        arrive(start)
        rows = layer_norm(block[start : start + GROUP].astype(F32), gain.reshape(1, 1, LANES), 2)
        rows = rows.astype(BF16)
        for i in range(GROUP):
            base = place_of(start + i)
            normed[base : base + SIDE, :] = rows[i]
            normed[base + SIDE : base + SLOT, :] = pad


def place_of(i):
    return (i % HALF) * LANES + (i // HALF) * SLOT


def project(normed, weight, staged, extra):
    wt = weight.astype(F32).T.astype(BF16)
    lane = lane_of(CH)
    for s in ORDER:
        proj = lax.dot_general(wt, normed[s * LANES : (s + 1) * LANES, :], NT, preferred_element_type=F32)
        left = sigmoid(proj[:CH]) * proj[CH : 2 * CH]
        right = sigmoid(proj[2 * CH : 3 * CH]) * proj[3 * CH :]
        first = jnp.where(lane < SLOT, left, pltpu.roll(right, SLOT, 1))
        second = jnp.where(lane < SLOT, pltpu.roll(left, SLOT, 1), right)
        if s + HALF >= MAIN:
            for g in range(SIDE // PIECE):
                extra[g * EXTRA + s + HALF - MAIN] = pltpu.roll(second, SIDE - g * PIECE, 1)
        else:
            staged[pl.ds((s + HALF) * STRIDE, CH), :] = jnp.where(lane % SLOT < SIDE, second, extra[s + HALF])
        staged[pl.ds(s * STRIDE, CH), :] = jnp.where(lane % SLOT < SIDE, first, extra[s])


ORDER = [*range(HALF - EXTRA, HALF), *range(HALF - EXTRA)]


def write_messages(staged, out):
    for channel in range(CH):
        for t in range(TILES):
            tile = staged[pl.ds(channel + t * TILE * STRIDE, TILE, stride=STRIDE), :]
            out[channel, :, t * LANES : (t + 1) * LANES] = tile.astype(BF16)


def project_kernel(pair_hbm, gain_hbm, weight_hbm, out, pair, gain, weight, sems, normed, staged, extra):
    groups = SIDE // GROUP
    copies = [pltpu.make_async_copy(gain_hbm, gain, sems.at[groups])]
    for n in range(groups):
        rows = pl.ds(n * GROUP, GROUP)
        copies.append(pltpu.make_async_copy(pair_hbm.at[rows], pair.at[rows], sems.at[n]))
    copies.append(pltpu.make_async_copy(weight_hbm.at[0], weight, sems.at[groups + 1]))
    for copy in copies:
        copy.start()
    copies[0].wait()
    normalize(pair, gain[0:1, :], normed, lambda start: copies[1 + start // GROUP].wait())
    copies[-1].wait()
    project(normed, weight[...], staged, extra)
    write_messages(staged, out)


def gate_kernel(p, pair, gain, gweight, gate, normed):
    normalize(pair, gain[p : p + 1, :], normed)
    for start in range(0, HALF * LANES, 4 * LANES):
        rows = slice(start, start + 4 * LANES)
        gate[rows, :] = sigmoid(jnp.dot(normed[rows, :], gweight[p], preferred_element_type=F32))


def read_sums(mixed, mixed32):
    for channel in range(CH):
        for t in range(KEPT // 2):
            tile = mixed[channel, :, t * LANES : (t + 1) * LANES].astype(F32)
            mixed32[pl.ds(channel * HALF + 2 * t, 2), :] = tile


def sums_of(mixed32, s):
    if s < KEPT:
        return mixed32[pl.ds(s, CH, stride=HALF), :]
    lane, sums = lane_of(CH) % SLOT, None
    for g in range(SIDE // PIECE):
        part = mixed32[pl.ds(g * (HALF - KEPT) + s - KEPT, CH, stride=HALF), :]
        part = pltpu.roll(part, LANES - SIDE + g * PIECE, 1)
        sums = part if sums is None else jnp.where(lane < g * PIECE, sums, part)
    return sums


def finish(pair, gate, mixed, hgain, oweight, z_out, mixed32, hidden, ready=lambda s: None):
    hcol = hgain.T
    read_sums(mixed, mixed32)
    for s in range(0, HALF, 4):
        sums = [sums_of(mixed32, s + t) for t in range(4)]
        sums = [layer_norm(values, hcol, 0).astype(BF16) for values in sums]
        for t in range(4):
            hidden[s + t] = sums[t]
    for s in range(0, HALF, 4):
        updates = [
            lax.dot_general(hidden[s + t], oweight, TN, preferred_element_type=F32) for t in range(4)
        ]
        change = gate[s * LANES : (s + 4) * LANES, :] * jnp.concatenate(updates, axis=0)
        for h in range(2):
            old = [pair[s + t + h * HALF].astype(F32) for t in range(4)]
            new = [
                old[t] + change[t * LANES + h * SLOT : t * LANES + h * SLOT + SIDE] for t in range(4)
            ]
            for t in range(4):
                z_out[s + t + h * HALF] = new[t].astype(BF16)
            ready(s + h * HALF)


def middle_kernel(
    pair, gate, mixed, gain, hgain, oweight, weight, z_out, out, normed, mixed32, hidden, staged, extra
):
    finish(pair, gate, mixed, hgain[0:1, :], oweight[0], z_out, mixed32, hidden)
    normalize(z_out, gain[1:2, :], normed)
    project(normed, weight[1], staged, extra)
    write_messages(staged, out)


def last_kernel(pair, gate, mixed, hgain, oweight, z_hbm, z_out, sems, mixed32, hidden):
    copies = []

    def ready(s):
        rows = pl.ds(s, 4)
        copies.append(pltpu.make_async_copy(z_out.at[rows], z_hbm.at[rows], sems.at[s // 4]))
        copies[-1].start()

    finish(pair, gate, mixed, hgain[1:2, :], oweight[1], z_out, mixed32, hidden, ready)
    for copy in copies:
        copy.wait()


def moved(got, p, base, offset):
    values = got[p].astype(F32)
    tiles = [values[:, t * LANES : (t + 1) * LANES] for t in range(TILES)]
    main = rolled(jnp.concatenate(tiles, axis=0), offset - base)
    first = rest = None
    for g in range(SIDE // PIECE):
        begin = offset + g * PIECE
        shift = begin - base - SIDE
        head = rolled(tiles[3 * g], shift)
        tail = rolled(jnp.concatenate(tiles[3 * g + 1 : 3 * g + 3], axis=0), shift)
        if g == 0:
            first, rest = head, tail
        else:
            first = jnp.where((lane_of(TILE) - begin) % LANES < PIECE, head, first)
            rest = jnp.where((lane_of(2 * TILE) - begin) % LANES < PIECE, tail, rest)
    return jnp.concatenate([main, first, rest], axis=0)


def rolled(values, shift):
    return pltpu.roll(values, shift % LANES, 1) if shift % LANES else values


def dense(ref, which, base):
    lane = lane_of(SIDE)
    tiles = [None] * 3
    for b, p in enumerate(which):
        first, offset = divmod(b * SIDE, LANES)
        block = moved(ref, p, base, offset)
        tiles[first] = block if offset == 0 else jnp.where(lane < offset, tiles[first], block)
        if offset + SIDE > LANES:
            tiles[first + 1] = block
    return jnp.concatenate(tiles, axis=1).astype(BF16)


def out_right_kernel(got, me, right):
    for a in range(4):
        for n, core in enumerate((me[0], 1 - me[0])):
            start = n * 192 + a * SIDE
            right[start : start + SIDE, :] = dense(got, [(2 * a + core) * 8 + b for b in range(8)], SLOT)


def out_left_kernel(got, left):
    for a in range(8):
        left[a * SIDE : (a + 1) * SIDE, :] = dense(got, [a * 8 + b for b in range(8)], 0)


def send_back(total, blocks, place, out):
    lane = lane_of(HALF)
    for a in range(blocks):
        for b in range(0, 4, 2):
            tile = total[a * SIDE : (a + 1) * SIDE, b * SLOT : (b + 2) * SLOT]
            low, high = tile[:HALF], tile[HALF:]
            write_sums(jnp.where(lane < SLOT, low, pltpu.roll(high, SLOT, 1)), place(a, b), out)
            write_sums(jnp.where(lane < SLOT, pltpu.roll(low, SLOT, 1), high), place(a, b + 1), out)


def write_sums(rows, p, out):
    last = rows[16:]
    spare = [pltpu.roll(last, SIDE - g * PIECE, 1)[KEPT - 16 :] for g in range(SIDE // PIECE)]
    lane = lane_of(KEPT) % SLOT
    rows = jnp.where(lane < SIDE, rows[:KEPT], jnp.concatenate(spare, axis=0)).astype(BF16)
    for t in range(KEPT // 2):
        out[p, :, t * LANES : (t + 1) * LANES] = rows[2 * t : 2 * t + 2]


def padded(ref, start):
    pad = jnp.zeros((SLOT - SIDE, ref.shape[1]), BF16)
    pieces = []
    for b in range(4):
        pieces += [ref[start + b * SIDE : start + (b + 1) * SIDE, :], pad]
    return jnp.concatenate(pieces, axis=0)


def mix_out_kernel(left, left_c, right, right_c, right_y, right_yc, me, out):
    for step, (near, far) in enumerate(((right, right_c), (right_y, right_yc))):
        total = lax.dot_general(left[...], padded(near, 0), NT, preferred_element_type=F32)
        total += lax.dot_general(left_c[...], padded(far, 192), NT, preferred_element_type=F32)
        owner = me[0] if step == 0 else 1 - me[0]
        send_back(total, 8, lambda a, b: a * 8 + (2 * (b // 2) + owner) * 2 + b % 2, out)


def in_left_kernel(got, out, left):
    for r in range(8):
        rows = slice(r * SIDE, (r + 1) * SIDE)
        left[rows, :] = dense(got, [(r + 8 * h) * 4 + b for h in range(2) for b in range(4)], 0)
    out[...] = left[...].T


def in_right_kernel(got, right):
    lane = lane_of(SIDE)
    for r in range(16):
        for b in range(0, 4, 2):
            low, high = moved(got, r * 4 + b, SLOT, 0), moved(got, r * 4 + b + 1, SLOT, SLOT)
            tile = jnp.where(lane < SLOT, low, high)
            right[r * SIDE : (r + 1) * SIDE, b * SLOT : (b + 2) * SLOT] = tile.astype(BF16)


def mix_in_kernel(right, left, left_c, left_x, left_d, me, core, out):
    for step, ref in enumerate((left, left_c, left_x, left_d)):
        total = jnp.dot(ref[:192, :], right[:384, :], preferred_element_type=F32)
        total += jnp.dot(ref[192:, :], right[384:, :], preferred_element_type=F32)
        c = core[0] if step % 2 == 0 else 1 - core[0]
        low = me[0] if step < 2 else 1 - me[0]
        send_back(
            total,
            4,
            lambda a, b: (2 * (a // 2) + low) * 16 + (2 * (a % 2) + c) * 4 + b,
            out,
        )


def swap(values, *axes):
    n = 1 << len(axes)
    return lax.ppermute(values, axes, [(i, n - 1 - i) for i in range(n)])


MESSAGE = (CH, TILE, TILES * LANES)
EXTRAS = (MAIN, CH, LANES)
BACK = (CH, 2, KEPT // 2 * LANES)
BLOCK = (SIDE, SIDE, LANES)
GATE = (HALF * LANES, LANES)


def body(pair, norm_gain, proj_weight, hid_gain, out_weight, gate_weight):
    normed = pltpu.VMEM(GATE, BF16)
    staged = pltpu.VMEM((MAIN * STRIDE, LANES), F32)
    extra = pltpu.VMEM(EXTRAS, F32)
    mixed32 = pltpu.VMEM((CH * HALF, LANES), F32)
    hidden = pltpu.VMEM((HALF, CH, LANES), BF16)
    block = pltpu.VMEM(BLOCK, BF16)
    gain32, weight = pltpu.VMEM((2, LANES), F32), pltpu.VMEM((LANES, 4 * CH), BF16)
    out_axes, in_axes = ("yh", "zl", "xh", "xl", "zh"), ("yh", "yl", "zl", "xh", "zh")
    tie = lax.optimization_barrier
    pair, core, low_y, low_x = tie((pair, *(lax.axis_index(name).reshape(1) for name in ("c", "yl", "xl"))))

    (sent,) = call(
        project_kernel,
        [MESSAGE],
        3,
        [block, gain32, weight, pltpu.SemaphoreType.DMA((SIDE // GROUP + 2,)), normed, staged, extra],
        inputs=HBM,
        limit=55 << 20,
    )(pair, norm_gain, proj_weight)
    got = lax.all_to_all(sent, out_axes, 0, 0, tiled=True)
    (right,) = call(out_right_kernel, [(384, 384)], 1, smem=1)(got, core)
    right_y, right_c = swap(right, "yl"), swap(right, "c")
    got, right = tie((got, right))
    (left,) = call(out_left_kernel, [(384, 384)], 1)(got)
    left_c = swap(left, "c")
    source, left = tie((pair, left))
    (gate,) = call(functools.partial(gate_kernel, 0), [GATE], 3, [normed], dtype=F32)(source, norm_gain, gate_weight)
    right_y, gate = tie((right_y, gate))
    (sent,) = call(mix_out_kernel, [BACK], 6, smem=1)(
        left, left_c, right, right_c, right_y, swap(right_y, "c"), low_y
    )
    mixed = lax.all_to_all(sent, out_axes, 0, 0, tiled=True)
    first, sent = call(middle_kernel, [BLOCK, MESSAGE], 7, [normed, mixed32, hidden, staged, extra])(
        pair, gate, mixed, norm_gain, hid_gain, out_weight, proj_weight
    )
    got = lax.all_to_all(sent, in_axes, 0, 0, tiled=True)
    (left,) = call(in_left_kernel, [(384, 384)], 1, [pltpu.VMEM((384, 384), BF16)])(got)
    left_x, left_c = swap(left, "xl"), swap(left, "c")
    got, left = tie((got, left))
    (right,) = call(in_right_kernel, [(768, 256)], 1)(got)
    source, right = tie((first, right))
    (gate,) = call(functools.partial(gate_kernel, 1), [GATE], 3, [normed], dtype=F32)(source, norm_gain, gate_weight)
    left_x, gate = tie((left_x, gate))
    (sent,) = call(mix_in_kernel, [BACK], 5, smem=2)(right, left, left_c, left_x, swap(left_x, "c"), low_x, core)
    mixed = lax.all_to_all(sent, in_axes, 0, 0, tiled=True)
    (updated,) = call(
        last_kernel,
        [BLOCK],
        5,
        [block, pltpu.SemaphoreType.DMA((SIDE // 4,)), mixed32, hidden],
        outputs=HBM,
    )(first, gate, mixed, hid_gain, out_weight)
    return updated


def solution(mesh):
    names = ("yh", "yl", "zl", "xh", "xl", "zh", "c")
    fine = Mesh(mesh.devices.reshape(2, 2, 4, 2, 2, 2, 2), names)
    spec = P(names[:3], names[3:], None)
    return jax.shard_map(
        body,
        mesh=fine,
        in_specs=(spec, P(), P(), P(), P(), P()),
        out_specs=spec,
        check_vma=False,
    )
```

```python
import functools

import jax
import jax.numpy as jnp
from jax import lax
from jax.experimental import pallas as pl
from jax.experimental.pallas import tpu as pltpu
from jax.sharding import Mesh
from jax.sharding import PartitionSpec as P

F32, BF16 = jnp.float32, jnp.bfloat16
SIDE = 48
HALF = SIDE // 2
SLOT = 64
MAIN = 36
TILE = 4
TILES = MAIN // TILE
EXTRA = SIDE - MAIN
STRIDE = 72
GROUP = 16
KEPT = 18
PIECE = 16
CH = 64
LANES = 128
EPS = 1e-05
NT = (((1,), (1,)), ((), ()))
TN = (((0,), (0,)), ((), ()))
VMEM = pl.BlockSpec(memory_space=pltpu.VMEM)
SMEM = pl.BlockSpec(memory_space=pltpu.SMEM)
HBM = pl.BlockSpec(memory_space=pltpu.HBM)


def call(kernel, outs, n_in, scratch=(), smem=0, inputs=VMEM, outputs=VMEM, dtype=BF16, pin=False):
    return pl.pallas_call(
        kernel,
        out_shape=[(pltpu.VMEM if pin else jax.ShapeDtypeStruct)(shape, dtype) for shape in outs],
        in_specs=[inputs] * n_in + [SMEM] * smem,
        out_specs=[outputs] * len(outs),
        scratch_shapes=scratch,
        compiler_params=pltpu.CompilerParams(vmem_limit_bytes=16 << 20),
    )


def lane_of(rows):
    return lax.broadcasted_iota(jnp.int32, (rows, LANES), 1)


def layer_norm(values, gain, axis):
    mean = jnp.mean(values, axis=axis, keepdims=True)
    centred = values - mean
    var = jnp.mean(centred * centred, axis=axis, keepdims=True)
    return centred * lax.rsqrt(var + EPS) * gain


def sigmoid(values):
    return 0.5 * jnp.tanh(0.5 * values) + 0.5


def normalize(block, gain, normed, arrive=lambda start: None):
    pad = jnp.zeros((SLOT - SIDE, LANES), BF16)
    for start in range(0, SIDE, GROUP):
        arrive(start)
        rows = layer_norm(block[start : start + GROUP].astype(F32), gain.reshape(1, 1, LANES), 2)
        rows = rows.astype(BF16)
        for i in range(GROUP):
            base = place_of(start + i)
            normed[base : base + SIDE, :] = rows[i]
            normed[base + SIDE : base + SLOT, :] = pad


def place_of(i):
    return (i % HALF) * LANES + (i // HALF) * SLOT


def project(normed, weight, staged, extra):
    wt = weight.astype(F32).T.astype(BF16)
    lane = lane_of(CH)
    for s in ORDER:
        proj = lax.dot_general(wt, normed[s * LANES : (s + 1) * LANES, :], NT, preferred_element_type=F32)
        left = sigmoid(proj[:CH]) * proj[CH : 2 * CH]
        right = sigmoid(proj[2 * CH : 3 * CH]) * proj[3 * CH :]
        first = jnp.where(lane < SLOT, left, pltpu.roll(right, SLOT, 1))
        second = jnp.where(lane < SLOT, pltpu.roll(left, SLOT, 1), right)
        if s + HALF >= MAIN:
            for g in range(SIDE // PIECE):
                extra[g * EXTRA + s + HALF - MAIN] = pltpu.roll(second, SIDE - g * PIECE, 1)
        else:
            staged[pl.ds((s + HALF) * STRIDE, CH), :] = jnp.where(lane % SLOT < SIDE, second, extra[s + HALF])
        staged[pl.ds(s * STRIDE, CH), :] = jnp.where(lane % SLOT < SIDE, first, extra[s])


ORDER = [*range(HALF - EXTRA, HALF), *range(HALF - EXTRA)]


def write_messages(staged, out):
    for channel in range(CH):
        for t in range(TILES):
            tile = staged[pl.ds(channel + t * TILE * STRIDE, TILE, stride=STRIDE), :]
            out[channel, :, t * LANES : (t + 1) * LANES] = tile.astype(BF16)


def project_kernel(pair_hbm, gain_hbm, weight_hbm, out, pair, gain, weight, sems, normed, staged, extra):
    groups = SIDE // GROUP
    copies = [pltpu.make_async_copy(gain_hbm, gain, sems.at[groups])]
    for n in range(groups):
        rows = pl.ds(n * GROUP, GROUP)
        copies.append(pltpu.make_async_copy(pair_hbm.at[rows], pair.at[rows], sems.at[n]))
    copies.append(pltpu.make_async_copy(weight_hbm.at[0], weight, sems.at[groups + 1]))
    for copy in copies:
        copy.start()
    copies[0].wait()
    normalize(pair, gain[0:1, :], normed, lambda start: copies[1 + start // GROUP].wait())
    copies[-1].wait()
    project(normed, weight[...], staged, extra)
    write_messages(staged, out)


def gate_kernel(p, pair, gain, gweight, gate, normed):
    normalize(pair, gain[p : p + 1, :], normed)
    for start in range(0, HALF * LANES, 4 * LANES):
        rows = slice(start, start + 4 * LANES)
        gate[rows, :] = sigmoid(jnp.dot(normed[rows, :], gweight[p], preferred_element_type=F32))


def read_sums(mixed, mixed32):
    for channel in range(CH):
        for t in range(KEPT // 2):
            tile = mixed[channel, :, t * LANES : (t + 1) * LANES].astype(F32)
            mixed32[pl.ds(channel * HALF + 2 * t, 2), :] = tile


def sums_of(mixed32, s):
    if s < KEPT:
        return mixed32[pl.ds(s, CH, stride=HALF), :]
    lane, sums = lane_of(CH) % SLOT, None
    for g in range(SIDE // PIECE):
        part = mixed32[pl.ds(g * (HALF - KEPT) + s - KEPT, CH, stride=HALF), :]
        part = pltpu.roll(part, LANES - SIDE + g * PIECE, 1)
        sums = part if sums is None else jnp.where(lane < g * PIECE, sums, part)
    return sums


def finish(pair, gate, mixed, hgain, oweight, z_out, mixed32, hidden, ready=lambda s: None):
    hcol = hgain.T
    read_sums(mixed, mixed32)
    for s in range(0, HALF, 4):
        sums = [sums_of(mixed32, s + t) for t in range(4)]
        sums = [layer_norm(values, hcol, 0).astype(BF16) for values in sums]
        for t in range(4):
            hidden[s + t] = sums[t]
    for s in range(0, HALF, 4):
        updates = [
            lax.dot_general(hidden[s + t], oweight, TN, preferred_element_type=F32) for t in range(4)
        ]
        change = gate[s * LANES : (s + 4) * LANES, :] * jnp.concatenate(updates, axis=0)
        for h in range(2):
            old = [pair[s + t + h * HALF].astype(F32) for t in range(4)]
            new = [
                old[t] + change[t * LANES + h * SLOT : t * LANES + h * SLOT + SIDE] for t in range(4)
            ]
            for t in range(4):
                z_out[s + t + h * HALF] = new[t].astype(BF16)
            ready(s + h * HALF)


def middle_kernel(
    pair, gate, mixed, gain, hgain, oweight, weight, z_out, out, normed, mixed32, hidden, staged, extra
):
    finish(pair, gate, mixed, hgain[0:1, :], oweight[0], z_out, mixed32, hidden)
    normalize(z_out, gain[1:2, :], normed)
    project(normed, weight[1], staged, extra)
    write_messages(staged, out)


def last_kernel(pair, gate, mixed, hgain, oweight, z_hbm, z_out, sems, mixed32, hidden):
    copies = []

    def ready(s):
        rows = pl.ds(s, 4)
        copies.append(pltpu.make_async_copy(z_out.at[rows], z_hbm.at[rows], sems.at[s // 4]))
        copies[-1].start()

    finish(pair, gate, mixed, hgain[1:2, :], oweight[1], z_out, mixed32, hidden, ready)
    for copy in copies:
        copy.wait()


def moved(got, p, base, offset):
    values = got[p].astype(F32)
    tiles = [values[:, t * LANES : (t + 1) * LANES] for t in range(TILES)]
    main = rolled(jnp.concatenate(tiles, axis=0), offset - base)
    first = rest = None
    for g in range(SIDE // PIECE):
        begin = offset + g * PIECE
        shift = begin - base - SIDE
        head = rolled(tiles[3 * g], shift)
        tail = rolled(jnp.concatenate(tiles[3 * g + 1 : 3 * g + 3], axis=0), shift)
        if g == 0:
            first, rest = head, tail
        else:
            first = jnp.where((lane_of(TILE) - begin) % LANES < PIECE, head, first)
            rest = jnp.where((lane_of(2 * TILE) - begin) % LANES < PIECE, tail, rest)
    return jnp.concatenate([main, first, rest], axis=0)


def rolled(values, shift):
    return pltpu.roll(values, shift % LANES, 1) if shift % LANES else values


def dense(ref, which, base):
    lane = lane_of(SIDE)
    tiles = [None] * 3
    for b, p in enumerate(which):
        first, offset = divmod(b * SIDE, LANES)
        block = moved(ref, p, base, offset)
        tiles[first] = block if offset == 0 else jnp.where(lane < offset, tiles[first], block)
        if offset + SIDE > LANES:
            tiles[first + 1] = block
    return jnp.concatenate(tiles, axis=1).astype(BF16)


def out_right_kernel(got, me, right):
    for a in range(4):
        for n, core in enumerate((me[0], 1 - me[0])):
            start = n * 192 + a * SIDE
            right[start : start + SIDE, :] = dense(got, [(2 * a + core) * 8 + b for b in range(8)], SLOT)


def out_left_kernel(got, left):
    for a in range(8):
        left[a * SIDE : (a + 1) * SIDE, :] = dense(got, [a * 8 + b for b in range(8)], 0)


def send_back(total, blocks, place, out):
    lane = lane_of(HALF)
    for a in range(blocks):
        for b in range(0, 4, 2):
            tile = total[a * SIDE : (a + 1) * SIDE, b * SLOT : (b + 2) * SLOT]
            low, high = tile[:HALF], tile[HALF:]
            write_sums(jnp.where(lane < SLOT, low, pltpu.roll(high, SLOT, 1)), place(a, b), out)
            write_sums(jnp.where(lane < SLOT, pltpu.roll(low, SLOT, 1), high), place(a, b + 1), out)


def write_sums(rows, p, out):
    last = rows[16:]
    spare = [pltpu.roll(last, SIDE - g * PIECE, 1)[KEPT - 16 :] for g in range(SIDE // PIECE)]
    lane = lane_of(KEPT) % SLOT
    rows = jnp.where(lane < SIDE, rows[:KEPT], jnp.concatenate(spare, axis=0)).astype(BF16)
    for t in range(KEPT // 2):
        out[p, :, t * LANES : (t + 1) * LANES] = rows[2 * t : 2 * t + 2]


def padded(ref, start):
    pad = jnp.zeros((SLOT - SIDE, ref.shape[1]), BF16)
    pieces = []
    for b in range(4):
        pieces += [ref[start + b * SIDE : start + (b + 1) * SIDE, :], pad]
    return jnp.concatenate(pieces, axis=0)


def out_sums(left, left_c, near, far, place, out):
    total = lax.dot_general(left[...], padded(near, 0), NT, preferred_element_type=F32)
    total += lax.dot_general(left_c[...], padded(far, 192), NT, preferred_element_type=F32)
    send_back(total, 8, place, out)


def out_early_kernel(left, left_c, right, right_c, out):
    out_sums(left, left_c, right, right_c, lambda a, b: a * 4 + b, out)


def out_late_kernel(left, left_c, right_y, right_yc, early, me, out):
    def place(owner):
        return lambda a, b: a * 8 + (2 * (b // 2) + owner) * 2 + b % 2

    for a in range(8):
        for b in range(4):
            out[place(me[0])(a, b)] = early[a * 4 + b]
    out_sums(left, left_c, right_y, right_yc, place(1 - me[0]), out)


def in_left_kernel(got, out, left):
    for r in range(8):
        rows = slice(r * SIDE, (r + 1) * SIDE)
        left[rows, :] = dense(got, [(r + 8 * h) * 4 + b for h in range(2) for b in range(4)], 0)
    out[...] = left[...].T


def in_right_kernel(got, right):
    lane = lane_of(SIDE)
    for r in range(16):
        for b in range(0, 4, 2):
            low, high = moved(got, r * 4 + b, SLOT, 0), moved(got, r * 4 + b + 1, SLOT, SLOT)
            tile = jnp.where(lane < SLOT, low, high)
            right[r * SIDE : (r + 1) * SIDE, b * SLOT : (b + 2) * SLOT] = tile.astype(BF16)


def in_sums(left, right, place, out):
    total = jnp.dot(left[:192, :], right[:384, :], preferred_element_type=F32)
    total += jnp.dot(left[192:, :], right[384:, :], preferred_element_type=F32)
    send_back(total, 4, place, out)


def in_early_kernel(right, left, left_c, left_x, out):
    for n, ref in enumerate((left, left_c, left_x)):
        in_sums(ref, right, lambda a, b: n * 16 + a * 4 + b, out)


def in_late_kernel(right, left_d, early, me, core, out):
    def place(low, c):
        return lambda a, b: (2 * (a // 2) + low) * 16 + (2 * (a % 2) + c) * 4 + b

    places = [(me[0], core[0]), (me[0], 1 - core[0]), (1 - me[0], core[0])]
    for n, at in enumerate(places):
        for a in range(4):
            for b in range(4):
                out[place(*at)(a, b)] = early[n * 16 + a * 4 + b]
    in_sums(left_d, right, place(1 - me[0], 1 - core[0]), out)


def swap(values, *axes):
    n = 1 << len(axes)
    return lax.ppermute(values, axes, [(i, n - 1 - i) for i in range(n)])


MESSAGE = (CH, TILE, TILES * LANES)
EXTRAS = (MAIN, CH, LANES)
BACK = (CH, 2, KEPT // 2 * LANES)
BLOCK = (SIDE, SIDE, LANES)
GATE = (HALF * LANES, LANES)


def body(pair, norm_gain, proj_weight, hid_gain, out_weight, gate_weight):
    normed = pltpu.VMEM(GATE, BF16)
    staged = pltpu.VMEM((MAIN * STRIDE, LANES), F32)
    extra = pltpu.VMEM(EXTRAS, F32)
    mixed32 = pltpu.VMEM((CH * HALF, LANES), F32)
    hidden = pltpu.VMEM((HALF, CH, LANES), BF16)
    block = pltpu.VMEM(BLOCK, BF16)
    gain32, weight = pltpu.VMEM((2, LANES), F32), pltpu.VMEM((LANES, 4 * CH), BF16)
    out_axes, in_axes = ("yh", "zl", "xh", "xl", "zh"), ("yh", "yl", "zl", "xh", "zh")
    tie = lax.optimization_barrier
    pair, core, low_y, low_x = tie((pair, *(lax.axis_index(name).reshape(1) for name in ("c", "yl", "xl"))))

    (sent,) = call(
        project_kernel,
        [MESSAGE],
        3,
        [block, gain32, weight, pltpu.SemaphoreType.DMA((SIDE // GROUP + 2,)), normed, staged, extra],
        inputs=HBM,
        pin=True,
    )(*(pltpu.with_memory_space_constraint(x, pltpu.HBM) for x in (pair, norm_gain, proj_weight)))
    got = lax.all_to_all(sent, out_axes, 0, 0, tiled=True)
    (right,) = call(out_right_kernel, [(384, 384)], 1, smem=1)(got, core)
    right_y, right_c = swap(right, "yl"), swap(right, "c")
    got, right = tie((got, right))
    (left,) = call(out_left_kernel, [(384, 384)], 1)(got)
    left_c = swap(left, "c")
    source, left = tie((pair, left))
    (gate,) = call(functools.partial(gate_kernel, 0), [GATE], 3, [normed], dtype=F32)(source, norm_gain, gate_weight)
    right_y, gate, left = tie((right_y, gate, left))
    (early,) = call(out_early_kernel, [(32, *BACK[1:])], 4)(left, left_c, right, right_c)
    (sent,) = call(out_late_kernel, [BACK], 5, smem=1)(
        left, left_c, right_y, swap(right_y, "c"), early, low_y
    )
    mixed = lax.all_to_all(sent, out_axes, 0, 0, tiled=True)
    first, sent = call(middle_kernel, [BLOCK, MESSAGE], 7, [normed, mixed32, hidden, staged, extra])(
        pair, gate, mixed, norm_gain, hid_gain, out_weight, proj_weight
    )
    got = lax.all_to_all(sent, in_axes, 0, 0, tiled=True)
    (left,) = call(in_left_kernel, [(384, 384)], 1, [pltpu.VMEM((384, 384), BF16)])(got)
    left_x, left_c = swap(left, "xl"), swap(left, "c")
    got, left = tie((got, left))
    (right,) = call(in_right_kernel, [(768, 256)], 1)(got)
    source, right = tie((first, right))
    (gate,) = call(functools.partial(gate_kernel, 1), [GATE], 3, [normed], dtype=F32)(source, norm_gain, gate_weight)
    left_x, gate, right = tie((left_x, gate, right))
    (early,) = call(in_early_kernel, [(48, *BACK[1:])], 4)(right, left, left_c, left_x)
    (sent,) = call(in_late_kernel, [BACK], 3, smem=2)(right, swap(left_x, "c"), early, low_x, core)
    mixed = lax.all_to_all(sent, in_axes, 0, 0, tiled=True)
    (updated,) = call(
        last_kernel,
        [BLOCK],
        5,
        [block, pltpu.SemaphoreType.DMA((SIDE // 4,)), mixed32, hidden],
        outputs=HBM,
    )(first, gate, mixed, hid_gain, out_weight)
    return updated


def solution(mesh):
    names = ("yh", "yl", "zl", "xh", "xl", "zh", "c")
    fine = Mesh(mesh.devices.reshape(2, 2, 4, 2, 2, 2, 2), names)
    spec = P(names[:3], names[3:], None)
    return jax.shard_map(
        body,
        mesh=fine,
        in_specs=(spec, P(), P(), P(), P(), P()),
        out_specs=spec,
        check_vma=False,
    )
```

```python
import functools

import jax
import jax.numpy as jnp
from jax import lax
from jax.experimental import pallas as pl
from jax.experimental.pallas import tpu as pltpu
from jax.sharding import Mesh
from jax.sharding import PartitionSpec as P

F32, BF16 = jnp.float32, jnp.bfloat16
SIDE = 48
HALF = SIDE // 2
SLOT = 64
MAIN = 36
TILE = 4
TILES = MAIN // TILE
EXTRA = SIDE - MAIN
STRIDE = 72
KEPT = 18
PIECE = 16
CH = 64
LANES = 128
EPS = 1e-05
NT = (((1,), (1,)), ((), ()))
TN = (((0,), (0,)), ((), ()))
VMEM = pl.BlockSpec(memory_space=pltpu.VMEM)
SMEM = pl.BlockSpec(memory_space=pltpu.SMEM)
HBM = pl.BlockSpec(memory_space=pltpu.HBM)


def call(kernel, outs, n_in, scratch=(), smem=0, inputs=VMEM, outputs=VMEM, dtype=BF16, pin=False):
    return pl.pallas_call(
        kernel,
        out_shape=[(pltpu.VMEM if pin else jax.ShapeDtypeStruct)(shape, dtype) for shape in outs],
        in_specs=[inputs] * n_in + [SMEM] * smem,
        out_specs=[outputs] * len(outs),
        scratch_shapes=scratch,
        compiler_params=pltpu.CompilerParams(vmem_limit_bytes=16 << 20),
    )


def lane_of(rows):
    return lax.broadcasted_iota(jnp.int32, (rows, LANES), 1)


def layer_norm(values, gain, axis):
    mean = jnp.mean(values, axis=axis, keepdims=True)
    centred = values - mean
    var = jnp.mean(centred * centred, axis=axis, keepdims=True)
    return centred * lax.rsqrt(var + EPS) * gain


def sigmoid(values):
    return 0.5 * jnp.tanh(0.5 * values) + 0.5


def normalize(block, gain, normed):
    pad = jnp.zeros((SLOT - SIDE, LANES), BF16)
    share = jnp.full((LANES, LANES), 1 / LANES, BF16)
    tokens = block[...].reshape(SIDE * SIDE, LANES)
    centred = tokens.astype(F32) - jnp.dot(tokens, share, preferred_element_type=F32)
    var = jnp.mean(centred * centred, axis=1, keepdims=True)
    rows = (centred * lax.rsqrt(var + EPS) * gain).astype(BF16)
    for i in range(SIDE):
        base = place_of(i)
        normed[base : base + SIDE, :] = rows[i * SIDE : (i + 1) * SIDE]
        normed[base + SIDE : base + SLOT, :] = pad


def place_of(i):
    return (i % HALF) * LANES + (i // HALF) * SLOT


def project(normed, weight, staged, extra):
    wt = weight.astype(F32).T.astype(BF16)
    lane = lane_of(CH)
    for s in ORDER:
        proj = lax.dot_general(wt, normed[s * LANES : (s + 1) * LANES, :], NT, preferred_element_type=F32)
        left = sigmoid(proj[:CH]) * proj[CH : 2 * CH]
        right = sigmoid(proj[2 * CH : 3 * CH]) * proj[3 * CH :]
        first = jnp.where(lane < SLOT, left, pltpu.roll(right, SLOT, 1))
        second = jnp.where(lane < SLOT, pltpu.roll(left, SLOT, 1), right)
        if s + HALF >= MAIN:
            for g in range(SIDE // PIECE):
                extra[g * EXTRA + s + HALF - MAIN] = pltpu.roll(second, SIDE - g * PIECE, 1)
        else:
            staged[pl.ds((s + HALF) * STRIDE, CH), :] = jnp.where(lane % SLOT < SIDE, second, extra[s + HALF])
        staged[pl.ds(s * STRIDE, CH), :] = jnp.where(lane % SLOT < SIDE, first, extra[s])


ORDER = [*range(HALF - EXTRA, HALF), *range(HALF - EXTRA)]


def write_messages(staged, out):
    for channel in range(CH):
        for t in range(TILES):
            tile = staged[pl.ds(channel + t * TILE * STRIDE, TILE, stride=STRIDE), :]
            out[channel, :, t * LANES : (t + 1) * LANES] = tile.astype(BF16)


def project_kernel(pair_hbm, gain_hbm, weight_hbm, out, pair, gain, weight, sems, normed, staged, extra):
    places = ((gain_hbm, gain), (pair_hbm, pair), (weight_hbm.at[0], weight))
    copies = [pltpu.make_async_copy(source, target, sems.at[n]) for n, (source, target) in enumerate(places)]
    for copy in copies:
        copy.start()
    for copy in copies:
        copy.wait()
    normalize(pair, gain[0:1, :], normed)
    project(normed, weight[...], staged, extra)
    write_messages(staged, out)


def gate_kernel(p, pair, gain, gweight, gate, normed):
    normalize(pair, gain[p : p + 1, :], normed)
    for start in range(0, HALF * LANES, 4 * LANES):
        rows = slice(start, start + 4 * LANES)
        gate[rows, :] = sigmoid(jnp.dot(normed[rows, :], gweight[p], preferred_element_type=F32))


def read_sums(mixed, mixed32):
    for channel in range(CH):
        for t in range(KEPT // 2):
            tile = mixed[channel, :, t * LANES : (t + 1) * LANES].astype(F32)
            mixed32[pl.ds(channel * HALF + 2 * t, 2), :] = tile


def sums_of(mixed32, s):
    if s < KEPT:
        return mixed32[pl.ds(s, CH, stride=HALF), :]
    lane, sums = lane_of(CH) % SLOT, None
    for g in range(SIDE // PIECE):
        part = mixed32[pl.ds(g * (HALF - KEPT) + s - KEPT, CH, stride=HALF), :]
        part = pltpu.roll(part, LANES - SIDE + g * PIECE, 1)
        sums = part if sums is None else jnp.where(lane < g * PIECE, sums, part)
    return sums


def finish(pair, gate, mixed, hgain, oweight, z_out, mixed32, hidden):
    hcol = hgain.T
    read_sums(mixed, mixed32)
    for s in range(0, HALF, 4):
        sums = [sums_of(mixed32, s + t) for t in range(4)]
        sums = [layer_norm(values, hcol, 0).astype(BF16) for values in sums]
        for t in range(4):
            hidden[s + t] = sums[t]
    for s in range(0, HALF, 4):
        updates = [
            lax.dot_general(hidden[s + t], oweight, TN, preferred_element_type=F32) for t in range(4)
        ]
        change = gate[s * LANES : (s + 4) * LANES, :] * jnp.concatenate(updates, axis=0)
        for h in range(2):
            old = [pair[s + t + h * HALF].astype(F32) for t in range(4)]
            new = [
                old[t] + change[t * LANES + h * SLOT : t * LANES + h * SLOT + SIDE] for t in range(4)
            ]
            for t in range(4):
                z_out[s + t + h * HALF] = new[t].astype(BF16)


def middle_kernel(
    pair, gate, mixed, gain, hgain, oweight, weight, z_out, out, normed, mixed32, hidden, staged, extra
):
    finish(pair, gate, mixed, hgain[0:1, :], oweight[0], z_out, mixed32, hidden)
    normalize(z_out, gain[1:2, :], normed)
    project(normed, weight[1], staged, extra)
    write_messages(staged, out)


def last_kernel(pair, gate, mixed, hgain, oweight, z_hbm, z_out, sem, mixed32, hidden):
    finish(pair, gate, mixed, hgain[1:2, :], oweight[1], z_out, mixed32, hidden)
    copy = pltpu.make_async_copy(z_out, z_hbm, sem)
    copy.start()
    copy.wait()


def moved(got, p, base, offset):
    values = got[p].astype(F32)
    tiles = [values[:, t * LANES : (t + 1) * LANES] for t in range(TILES)]
    main = rolled(jnp.concatenate(tiles, axis=0), offset - base)
    first = rest = None
    for g in range(SIDE // PIECE):
        begin = offset + g * PIECE
        shift = begin - base - SIDE
        head = rolled(tiles[3 * g], shift)
        tail = rolled(jnp.concatenate(tiles[3 * g + 1 : 3 * g + 3], axis=0), shift)
        if g == 0:
            first, rest = head, tail
        else:
            first = jnp.where((lane_of(TILE) - begin) % LANES < PIECE, head, first)
            rest = jnp.where((lane_of(2 * TILE) - begin) % LANES < PIECE, tail, rest)
    return jnp.concatenate([main, first, rest], axis=0)


def rolled(values, shift):
    return pltpu.roll(values, shift % LANES, 1) if shift % LANES else values


def dense(ref, which, base):
    lane = lane_of(SIDE)
    tiles = [None] * 3
    for b, p in enumerate(which):
        first, offset = divmod(b * SIDE, LANES)
        block = moved(ref, p, base, offset)
        tiles[first] = block if offset == 0 else jnp.where(lane < offset, tiles[first], block)
        if offset + SIDE > LANES:
            tiles[first + 1] = block
    return jnp.concatenate(tiles, axis=1).astype(BF16)


def out_right_kernel(got, me, right):
    for a in range(4):
        for n, core in enumerate((me[0], 1 - me[0])):
            start = n * 192 + a * SIDE
            right[start : start + SIDE, :] = dense(got, [(2 * a + core) * 8 + b for b in range(8)], SLOT)


def out_left_kernel(got, left):
    for a in range(8):
        left[a * SIDE : (a + 1) * SIDE, :] = dense(got, [a * 8 + b for b in range(8)], 0)


def send_back(total, blocks, place, out):
    lane = lane_of(HALF)
    for a in range(blocks):
        for b in range(0, 4, 2):
            tile = total[a * SIDE : (a + 1) * SIDE, b * SLOT : (b + 2) * SLOT]
            low, high = tile[:HALF], tile[HALF:]
            write_sums(jnp.where(lane < SLOT, low, pltpu.roll(high, SLOT, 1)), place(a, b), out)
            write_sums(jnp.where(lane < SLOT, pltpu.roll(low, SLOT, 1), high), place(a, b + 1), out)


def write_sums(rows, p, out):
    last = rows[16:]
    spare = [pltpu.roll(last, SIDE - g * PIECE, 1)[KEPT - 16 :] for g in range(SIDE // PIECE)]
    lane = lane_of(KEPT) % SLOT
    rows = jnp.where(lane < SIDE, rows[:KEPT], jnp.concatenate(spare, axis=0)).astype(BF16)
    for t in range(KEPT // 2):
        out[p, :, t * LANES : (t + 1) * LANES] = rows[2 * t : 2 * t + 2]


def padded(ref, start):
    pad = jnp.zeros((SLOT - SIDE, ref.shape[1]), BF16)
    pieces = []
    for b in range(4):
        pieces += [ref[start + b * SIDE : start + (b + 1) * SIDE, :], pad]
    return jnp.concatenate(pieces, axis=0)


def out_sums(left, left_c, near, far, place, out):
    total = lax.dot_general(left[...], padded(near, 0), NT, preferred_element_type=F32)
    total += lax.dot_general(left_c[...], padded(far, 192), NT, preferred_element_type=F32)
    send_back(total, 8, place, out)


def out_early_kernel(left, left_c, right, right_c, out):
    out_sums(left, left_c, right, right_c, lambda a, b: a * 4 + b, out)


def out_late_kernel(left, left_c, right_y, right_yc, early, me, out):
    def place(owner):
        return lambda a, b: a * 8 + (2 * (b // 2) + owner) * 2 + b % 2

    for a in range(8):
        for b in range(4):
            out[place(me[0])(a, b)] = early[a * 4 + b]
    out_sums(left, left_c, right_y, right_yc, place(1 - me[0]), out)


def in_left_kernel(got, out, left):
    for r in range(8):
        rows = slice(r * SIDE, (r + 1) * SIDE)
        left[rows, :] = dense(got, [(r + 8 * h) * 4 + b for h in range(2) for b in range(4)], 0)
    out[...] = left[...].T


def in_right_kernel(got, right):
    lane = lane_of(SIDE)
    for r in range(16):
        for b in range(0, 4, 2):
            low, high = moved(got, r * 4 + b, SLOT, 0), moved(got, r * 4 + b + 1, SLOT, SLOT)
            tile = jnp.where(lane < SLOT, low, high)
            right[r * SIDE : (r + 1) * SIDE, b * SLOT : (b + 2) * SLOT] = tile.astype(BF16)


def in_sums(left, right, place, out):
    total = jnp.dot(left[:192, :], right[:384, :], preferred_element_type=F32)
    total += jnp.dot(left[192:, :], right[384:, :], preferred_element_type=F32)
    send_back(total, 4, place, out)


def in_early_kernel(right, left, left_c, left_x, out):
    for n, ref in enumerate((left, left_c, left_x)):
        in_sums(ref, right, lambda a, b: n * 16 + a * 4 + b, out)


def in_late_kernel(right, left_d, early, me, core, out):
    def place(low, c):
        return lambda a, b: (2 * (a // 2) + low) * 16 + (2 * (a % 2) + c) * 4 + b

    places = [(me[0], core[0]), (me[0], 1 - core[0]), (1 - me[0], core[0])]
    for n, at in enumerate(places):
        for a in range(4):
            for b in range(4):
                out[place(*at)(a, b)] = early[n * 16 + a * 4 + b]
    in_sums(left_d, right, place(1 - me[0], 1 - core[0]), out)


def swap(values, *axes):
    n = 1 << len(axes)
    return lax.ppermute(values, axes, [(i, n - 1 - i) for i in range(n)])


MESSAGE = (CH, TILE, TILES * LANES)
EXTRAS = (MAIN, CH, LANES)
BACK = (CH, 2, KEPT // 2 * LANES)
BLOCK = (SIDE, SIDE, LANES)
GATE = (HALF * LANES, LANES)


def body(pair, norm_gain, proj_weight, hid_gain, out_weight, gate_weight):
    normed = pltpu.VMEM(GATE, BF16)
    staged = pltpu.VMEM((MAIN * STRIDE, LANES), F32)
    extra = pltpu.VMEM(EXTRAS, F32)
    mixed32 = pltpu.VMEM((CH * HALF, LANES), F32)
    hidden = pltpu.VMEM((HALF, CH, LANES), BF16)
    block = pltpu.VMEM(BLOCK, BF16)
    gain32, weight = pltpu.VMEM((2, LANES), F32), pltpu.VMEM((LANES, 4 * CH), BF16)
    out_axes, in_axes = ("yh", "zl", "xh", "xl", "zh"), ("yh", "yl", "zl", "xh", "zh")
    tie = lax.optimization_barrier
    pair, core, low_y, low_x = tie((pair, *(lax.axis_index(name).reshape(1) for name in ("c", "yl", "xl"))))

    (sent,) = call(
        project_kernel,
        [MESSAGE],
        3,
        [block, gain32, weight, pltpu.SemaphoreType.DMA((3,)), normed, staged, extra],
        inputs=HBM,
        pin=True,
    )(*(pltpu.with_memory_space_constraint(x, pltpu.HBM) for x in (pair, norm_gain, proj_weight)))
    got = lax.all_to_all(sent, out_axes, 0, 0, tiled=True)
    (right,) = call(out_right_kernel, [(384, 384)], 1, smem=1)(got, core)
    right_y, right_c = swap(right, "yl"), swap(right, "c")
    got, right = tie((got, right))
    (left,) = call(out_left_kernel, [(384, 384)], 1)(got)
    left_c = swap(left, "c")
    source, left = tie((pair, left))
    (gate,) = call(functools.partial(gate_kernel, 0), [GATE], 3, [normed], dtype=F32)(source, norm_gain, gate_weight)
    right_y, gate, left = tie((right_y, gate, left))
    (early,) = call(out_early_kernel, [(32, *BACK[1:])], 4)(left, left_c, right, right_c)
    (sent,) = call(out_late_kernel, [BACK], 5, smem=1)(
        left, left_c, right_y, swap(right_y, "c"), early, low_y
    )
    mixed = lax.all_to_all(sent, out_axes, 0, 0, tiled=True)
    first, sent = call(middle_kernel, [BLOCK, MESSAGE], 7, [normed, mixed32, hidden, staged, extra])(
        pair, gate, mixed, norm_gain, hid_gain, out_weight, proj_weight
    )
    got = lax.all_to_all(sent, in_axes, 0, 0, tiled=True)
    (left,) = call(in_left_kernel, [(384, 384)], 1, [pltpu.VMEM((384, 384), BF16)])(got)
    left_x, left_c = swap(left, "xl"), swap(left, "c")
    got, left = tie((got, left))
    (right,) = call(in_right_kernel, [(768, 256)], 1)(got)
    source, right = tie((first, right))
    (gate,) = call(functools.partial(gate_kernel, 1), [GATE], 3, [normed], dtype=F32)(source, norm_gain, gate_weight)
    left_x, gate, right = tie((left_x, gate, right))
    (early,) = call(in_early_kernel, [(48, *BACK[1:])], 4)(right, left, left_c, left_x)
    (sent,) = call(in_late_kernel, [BACK], 3, smem=2)(right, swap(left_x, "c"), early, low_x, core)
    mixed = lax.all_to_all(sent, in_axes, 0, 0, tiled=True)
    (updated,) = call(
        last_kernel,
        [BLOCK],
        5,
        [block, pltpu.SemaphoreType.DMA, mixed32, hidden],
        outputs=HBM,
    )(first, gate, mixed, hid_gain, out_weight)
    return updated


def solution(mesh):
    names = ("yh", "yl", "zl", "xh", "xl", "zh", "c")
    fine = Mesh(mesh.devices.reshape(2, 2, 4, 2, 2, 2, 2), names)
    spec = P(names[:3], names[3:], None)
    return jax.shard_map(
        body,
        mesh=fine,
        in_specs=(spec, P(), P(), P(), P(), P()),
        out_specs=spec,
        check_vma=False,
    )
```

```python
import functools

import jax
import jax.numpy as jnp
from jax import lax
from jax.experimental import pallas as pl
from jax.experimental.pallas import tpu as pltpu
from jax.sharding import Mesh
from jax.sharding import PartitionSpec as P

F32, BF16 = jnp.float32, jnp.bfloat16
SIDE = 48
HALF = SIDE // 2
SLOT = 64
MAIN = 36
TILE = 4
TILES = MAIN // TILE
EXTRA = SIDE - MAIN
STRIDE = 72
KEPT = 18
PIECE = 16
CH = 64
LANES = 128
EPS = 1e-05
NT = (((1,), (1,)), ((), ()))
TN = (((0,), (0,)), ((), ()))
VMEM = pl.BlockSpec(memory_space=pltpu.VMEM)
SMEM = pl.BlockSpec(memory_space=pltpu.SMEM)
HBM = pl.BlockSpec(memory_space=pltpu.HBM)


def call(kernel, outs, n_in, scratch=(), smem=0, inputs=VMEM, outputs=VMEM, dtype=BF16, pin=False):
    return pl.pallas_call(
        kernel,
        out_shape=[(pltpu.VMEM if pin else jax.ShapeDtypeStruct)(shape, dtype) for shape in outs],
        in_specs=[inputs] * n_in + [SMEM] * smem,
        out_specs=[outputs] * len(outs),
        scratch_shapes=scratch,
        compiler_params=pltpu.CompilerParams(vmem_limit_bytes=16 << 20),
    )


def lane_of(rows):
    return lax.broadcasted_iota(jnp.int32, (rows, LANES), 1)


def layer_norm(values, gain, axis):
    mean = jnp.mean(values, axis=axis, keepdims=True)
    centred = values - mean
    var = jnp.mean(centred * centred, axis=axis, keepdims=True)
    return centred * lax.rsqrt(var + EPS) * gain


def sigmoid(values):
    return 0.5 * jnp.tanh(0.5 * values) + 0.5


def normalize(block, gain, normed):
    pad = jnp.zeros((SLOT - SIDE, LANES), BF16)
    share = jnp.full((LANES, LANES), 1 / LANES, BF16)
    tokens = block[...].reshape(SIDE * SIDE, LANES)
    centred = tokens.astype(F32) - jnp.dot(tokens, share, preferred_element_type=F32)
    var = jnp.mean(centred * centred, axis=1, keepdims=True)
    rows = (centred * lax.rsqrt(var + EPS) * gain).astype(BF16)
    for i in range(SIDE):
        base = place_of(i)
        normed[base : base + SIDE, :] = rows[i * SIDE : (i + 1) * SIDE]
        normed[base + SIDE : base + SLOT, :] = pad


def place_of(i):
    return (i % HALF) * LANES + (i // HALF) * SLOT


def project(normed, weight, staged, extra):
    wt = weight.astype(F32).T.astype(BF16)
    lane = lane_of(CH)
    for s in ORDER:
        proj = lax.dot_general(wt, normed[s * LANES : (s + 1) * LANES, :], NT, preferred_element_type=F32)
        left = sigmoid(proj[:CH]) * proj[CH : 2 * CH]
        right = sigmoid(proj[2 * CH : 3 * CH]) * proj[3 * CH :]
        first = jnp.where(lane < SLOT, left, pltpu.roll(right, SLOT, 1))
        second = jnp.where(lane < SLOT, pltpu.roll(left, SLOT, 1), right)
        if s + HALF >= MAIN:
            for g in range(SIDE // PIECE):
                extra[g * EXTRA + s + HALF - MAIN] = pltpu.roll(second, SIDE - g * PIECE, 1)
        else:
            staged[pl.ds((s + HALF) * STRIDE, CH), :] = jnp.where(lane % SLOT < SIDE, second, extra[s + HALF])
        staged[pl.ds(s * STRIDE, CH), :] = jnp.where(lane % SLOT < SIDE, first, extra[s])


ORDER = [*range(HALF - EXTRA, HALF), *range(HALF - EXTRA)]


def write_messages(staged, out):
    for channel in range(CH):
        for t in range(TILES):
            tile = staged[pl.ds(channel + t * TILE * STRIDE, TILE, stride=STRIDE), :]
            out[channel, :, t * LANES : (t + 1) * LANES] = tile.astype(BF16)


def project_kernel(pair_hbm, gain_hbm, weight_hbm, out, pair, gain, weight, sems, normed, staged, extra):
    places = ((gain_hbm, gain), (pair_hbm, pair), (weight_hbm.at[0], weight))
    copies = [pltpu.make_async_copy(source, target, sems.at[n]) for n, (source, target) in enumerate(places)]
    for copy in copies:
        copy.start()
    for copy in copies:
        copy.wait()
    normalize(pair, gain[0:1, :], normed)
    project(normed, weight[...], staged, extra)
    write_messages(staged, out)


def gate_kernel(p, pair, gain, gweight, gate, normed):
    normalize(pair, gain[p : p + 1, :], normed)
    for start in range(0, HALF * LANES, 4 * LANES):
        rows = slice(start, start + 4 * LANES)
        gate[rows, :] = sigmoid(jnp.dot(normed[rows, :], gweight[p], preferred_element_type=F32))


def read_sums(mixed, mixed32):
    for channel in range(CH):
        for t in range(KEPT // 2):
            tile = mixed[channel, :, t * LANES : (t + 1) * LANES].astype(F32)
            mixed32[pl.ds(channel * HALF + 2 * t, 2), :] = tile


def sums_of(mixed32, s):
    if s < KEPT:
        return mixed32[pl.ds(s, CH, stride=HALF), :]
    lane, sums = lane_of(CH) % SLOT, None
    for g in range(SIDE // PIECE):
        part = mixed32[pl.ds(g * (HALF - KEPT) + s - KEPT, CH, stride=HALF), :]
        part = pltpu.roll(part, LANES - SIDE + g * PIECE, 1)
        sums = part if sums is None else jnp.where(lane < g * PIECE, sums, part)
    return sums


def finish(pair, gate, mixed, hgain, oweight, z_out, mixed32, hidden, ready=lambda s: None):
    hcol = hgain.T
    read_sums(mixed, mixed32)
    for s in range(0, HALF, 4):
        sums = [sums_of(mixed32, s + t) for t in range(4)]
        sums = [layer_norm(values, hcol, 0).astype(BF16) for values in sums]
        for t in range(4):
            hidden[s + t] = sums[t]
    for s in range(0, HALF, 4):
        updates = [
            lax.dot_general(hidden[s + t], oweight, TN, preferred_element_type=F32) for t in range(4)
        ]
        change = gate[s * LANES : (s + 4) * LANES, :] * jnp.concatenate(updates, axis=0)
        for h in range(2):
            old = [pair[s + t + h * HALF].astype(F32) for t in range(4)]
            new = [
                old[t] + change[t * LANES + h * SLOT : t * LANES + h * SLOT + SIDE] for t in range(4)
            ]
            for t in range(4):
                z_out[s + t + h * HALF] = new[t].astype(BF16)
        ready(s + 4)


def middle_kernel(
    pair, gate, mixed, gain, hgain, oweight, weight, z_out, out, normed, mixed32, hidden, staged, extra
):
    finish(pair, gate, mixed, hgain[0:1, :], oweight[0], z_out, mixed32, hidden)
    normalize(z_out, gain[1:2, :], normed)
    project(normed, weight[1], staged, extra)
    write_messages(staged, out)


def last_kernel(pair, gate, mixed, hgain, oweight, z_hbm, z_out, sems, mixed32, hidden):
    copies = []

    def ready(s):
        for start in (s - HALF // 2, s + HALF // 2) if s % (HALF // 2) == 0 else ():
            rows = pl.ds(start, HALF // 2)
            copies.append(pltpu.make_async_copy(z_out.at[rows], z_hbm.at[rows], sems.at[len(copies)]))
            copies[-1].start()

    finish(pair, gate, mixed, hgain[1:2, :], oweight[1], z_out, mixed32, hidden, ready)
    for copy in copies:
        copy.wait()


def moved(got, p, base, offset):
    values = got[p].astype(F32)
    tiles = [values[:, t * LANES : (t + 1) * LANES] for t in range(TILES)]
    main = rolled(jnp.concatenate(tiles, axis=0), offset - base)
    first = rest = None
    for g in range(SIDE // PIECE):
        begin = offset + g * PIECE
        shift = begin - base - SIDE
        head = rolled(tiles[3 * g], shift)
        tail = rolled(jnp.concatenate(tiles[3 * g + 1 : 3 * g + 3], axis=0), shift)
        if g == 0:
            first, rest = head, tail
        else:
            first = jnp.where((lane_of(TILE) - begin) % LANES < PIECE, head, first)
            rest = jnp.where((lane_of(2 * TILE) - begin) % LANES < PIECE, tail, rest)
    return jnp.concatenate([main, first, rest], axis=0)


def rolled(values, shift):
    return pltpu.roll(values, shift % LANES, 1) if shift % LANES else values


def dense(ref, which, base):
    lane = lane_of(SIDE)
    tiles = [None] * 3
    for b, p in enumerate(which):
        first, offset = divmod(b * SIDE, LANES)
        block = moved(ref, p, base, offset)
        tiles[first] = block if offset == 0 else jnp.where(lane < offset, tiles[first], block)
        if offset + SIDE > LANES:
            tiles[first + 1] = block
    return jnp.concatenate(tiles, axis=1).astype(BF16)


def out_right_kernel(got, me, right):
    for a in range(4):
        for n, core in enumerate((me[0], 1 - me[0])):
            start = n * 192 + a * SIDE
            right[start : start + SIDE, :] = dense(got, [(2 * a + core) * 8 + b for b in range(8)], SLOT)


def out_left_kernel(got, left):
    for a in range(8):
        left[a * SIDE : (a + 1) * SIDE, :] = dense(got, [a * 8 + b for b in range(8)], 0)


def send_back(total, blocks, place, out):
    lane = lane_of(HALF)
    for a in range(blocks):
        for b in range(0, 4, 2):
            tile = total[a * SIDE : (a + 1) * SIDE, b * SLOT : (b + 2) * SLOT]
            low, high = tile[:HALF], tile[HALF:]
            write_sums(jnp.where(lane < SLOT, low, pltpu.roll(high, SLOT, 1)), place(a, b), out)
            write_sums(jnp.where(lane < SLOT, pltpu.roll(low, SLOT, 1), high), place(a, b + 1), out)


def write_sums(rows, p, out):
    last = rows[16:]
    spare = [pltpu.roll(last, SIDE - g * PIECE, 1)[KEPT - 16 :] for g in range(SIDE // PIECE)]
    lane = lane_of(KEPT) % SLOT
    rows = jnp.where(lane < SIDE, rows[:KEPT], jnp.concatenate(spare, axis=0))
    for t in range(KEPT // 2):
        out[p, :, t * LANES : (t + 1) * LANES] = rows[2 * t : 2 * t + 2].astype(BF16)


def padded(ref, start):
    pad = jnp.zeros((SLOT - SIDE, ref.shape[1]), BF16)
    pieces = []
    for b in range(4):
        pieces += [ref[start + b * SIDE : start + (b + 1) * SIDE, :], pad]
    return jnp.concatenate(pieces, axis=0)


def out_sums(left, left_c, near, far, place, out):
    total = lax.dot_general(left[...], padded(near, 0), NT, preferred_element_type=F32)
    total += lax.dot_general(left_c[...], padded(far, 192), NT, preferred_element_type=F32)
    send_back(total, 8, place, out)


def out_early_kernel(left, left_c, right, right_c, out):
    out_sums(left, left_c, right, right_c, lambda a, b: a * 4 + b, out)


def out_late_kernel(left, left_c, right_y, right_yc, early, me, out):
    def place(owner):
        return lambda a, b: a * 8 + (2 * (b // 2) + owner) * 2 + b % 2

    for a in range(8):
        for b in range(4):
            out[place(me[0])(a, b)] = early[a * 4 + b]
    out_sums(left, left_c, right_y, right_yc, place(1 - me[0]), out)


def in_left_kernel(got, out, left):
    for r in range(8):
        rows = slice(r * SIDE, (r + 1) * SIDE)
        left[rows, :] = dense(got, [(r + 8 * h) * 4 + b for h in range(2) for b in range(4)], 0)
    out[...] = left[...].T


def in_right_kernel(got, right):
    lane = lane_of(SIDE)
    for r in range(16):
        for b in range(0, 4, 2):
            low, high = moved(got, r * 4 + b, SLOT, 0), moved(got, r * 4 + b + 1, SLOT, SLOT)
            tile = jnp.where(lane < SLOT, low, high)
            right[r * SIDE : (r + 1) * SIDE, b * SLOT : (b + 2) * SLOT] = tile.astype(BF16)


def in_sums(left, right, place, out):
    total = jnp.dot(left[:192, :], right[:384, :], preferred_element_type=F32)
    total += jnp.dot(left[192:, :], right[384:, :], preferred_element_type=F32)
    send_back(total, 4, place, out)


def in_early_kernel(right, left, left_c, left_x, out):
    for n, ref in enumerate((left, left_c, left_x)):
        in_sums(ref, right, lambda a, b: n * 16 + a * 4 + b, out)


def in_late_kernel(right, left_d, early, me, core, out):
    def place(low, c):
        return lambda a, b: (2 * (a // 2) + low) * 16 + (2 * (a % 2) + c) * 4 + b

    places = [(me[0], core[0]), (me[0], 1 - core[0]), (1 - me[0], core[0])]
    for n, at in enumerate(places):
        for a in range(4):
            for b in range(4):
                out[place(*at)(a, b)] = early[n * 16 + a * 4 + b]
    in_sums(left_d, right, place(1 - me[0], 1 - core[0]), out)


def swap(values, *axes):
    n = 1 << len(axes)
    return lax.ppermute(values, axes, [(i, n - 1 - i) for i in range(n)])


MESSAGE = (CH, TILE, TILES * LANES)
EXTRAS = (MAIN, CH, LANES)
BACK = (CH, 2, KEPT // 2 * LANES)
BLOCK = (SIDE, SIDE, LANES)
GATE = (HALF * LANES, LANES)


def body(pair, norm_gain, proj_weight, hid_gain, out_weight, gate_weight):
    normed = pltpu.VMEM(GATE, BF16)
    staged = pltpu.VMEM(((MAIN + 1) * STRIDE, LANES), F32)
    extra = pltpu.VMEM(EXTRAS, F32)
    mixed32 = pltpu.VMEM(((CH + 1) * HALF, LANES), F32)
    hidden = pltpu.VMEM((HALF, CH, LANES), BF16)
    block = pltpu.VMEM(BLOCK, BF16)
    gain32, weight = pltpu.VMEM((2, LANES), F32), pltpu.VMEM((LANES, 4 * CH), BF16)
    out_axes, in_axes = ("yh", "zl", "xh", "xl", "zh"), ("yh", "yl", "zl", "xh", "zh")
    tie = lax.optimization_barrier
    pair, core, low_y, low_x = tie((pair, *(lax.axis_index(name).reshape(1) for name in ("c", "yl", "xl"))))

    (sent,) = call(
        project_kernel,
        [MESSAGE],
        3,
        [block, gain32, weight, pltpu.SemaphoreType.DMA((3,)), normed, staged, extra],
        inputs=HBM,
        pin=True,
    )(*(pltpu.with_memory_space_constraint(x, pltpu.HBM) for x in (pair, norm_gain, proj_weight)))
    got = lax.all_to_all(sent, out_axes, 0, 0, tiled=True)
    (right,) = call(out_right_kernel, [(384, 384)], 1, smem=1)(got, core)
    right_y, right_c = swap(right, "yl"), swap(right, "c")
    got, right = tie((got, right))
    (left,) = call(out_left_kernel, [(384, 384)], 1)(got)
    left_c = swap(left, "c")
    source, left = tie((pair, left))
    (gate,) = call(functools.partial(gate_kernel, 0), [GATE], 3, [normed], dtype=F32)(source, norm_gain, gate_weight)
    right_y, gate, left = tie((right_y, gate, left))
    (early,) = call(out_early_kernel, [(32, *BACK[1:])], 4)(left, left_c, right, right_c)
    (sent,) = call(out_late_kernel, [BACK], 5, smem=1)(
        left, left_c, right_y, swap(right_y, "c"), early, low_y
    )
    mixed = lax.all_to_all(sent, out_axes, 0, 0, tiled=True)
    first, sent = call(middle_kernel, [BLOCK, MESSAGE], 7, [normed, mixed32, hidden, staged, extra])(
        pair, gate, mixed, norm_gain, hid_gain, out_weight, proj_weight
    )
    got = lax.all_to_all(sent, in_axes, 0, 0, tiled=True)
    (left,) = call(in_left_kernel, [(384, 384)], 1, [pltpu.VMEM((384, 384), BF16)])(got)
    left_x, left_c = swap(left, "xl"), swap(left, "c")
    got, left = tie((got, left))
    (right,) = call(in_right_kernel, [(768, 256)], 1)(got)
    source, right = tie((first, right))
    (gate,) = call(functools.partial(gate_kernel, 1), [GATE], 3, [normed], dtype=F32)(source, norm_gain, gate_weight)
    left_x, gate, right = tie((left_x, gate, right))
    (early,) = call(in_early_kernel, [(48, *BACK[1:])], 4)(right, left, left_c, left_x)
    (sent,) = call(in_late_kernel, [BACK], 3, smem=2)(right, swap(left_x, "c"), early, low_x, core)
    mixed = lax.all_to_all(sent, in_axes, 0, 0, tiled=True)
    (updated,) = call(
        last_kernel,
        [BLOCK],
        5,
        [block, pltpu.SemaphoreType.DMA((4,)), mixed32, hidden],
        outputs=HBM,
    )(first, gate, mixed, hid_gain, out_weight)
    return updated


def solution(mesh):
    names = ("yh", "yl", "zl", "xh", "xl", "zh", "c")
    fine = Mesh(mesh.devices.reshape(2, 2, 4, 2, 2, 2, 2), names)
    spec = P(names[:3], names[3:], None)
    return jax.shard_map(
        body,
        mesh=fine,
        in_specs=(spec, P(), P(), P(), P(), P()),
        out_specs=spec,
        check_vma=False,
    )
```

```python
import functools

import jax
import jax.numpy as jnp
from jax import lax
from jax.experimental import pallas as pl
from jax.experimental.pallas import tpu as pltpu
from jax.sharding import Mesh
from jax.sharding import PartitionSpec as P

F32, BF16 = jnp.float32, jnp.bfloat16
SIDE = 48
HALF = SIDE // 2
SLOT = 64
MAIN = 36
TILE = 4
TILES = MAIN // TILE
EXTRA = SIDE - MAIN
STRIDE = 72
KEPT = 18
PIECE = 16
CH = 64
LANES = 128
EPS = 1e-05
NT = (((1,), (1,)), ((), ()))
TN = (((0,), (0,)), ((), ()))
VMEM = pl.BlockSpec(memory_space=pltpu.VMEM)
SMEM = pl.BlockSpec(memory_space=pltpu.SMEM)
HBM = pl.BlockSpec(memory_space=pltpu.HBM)


def call(kernel, outs, n_in, scratch=(), smem=0, inputs=VMEM, outputs=VMEM, dtype=BF16, pin=False):
    return pl.pallas_call(
        kernel,
        out_shape=[(pltpu.VMEM if pin else jax.ShapeDtypeStruct)(shape, dtype) for shape in outs],
        in_specs=[inputs] * n_in + [SMEM] * smem,
        out_specs=[outputs] * len(outs),
        scratch_shapes=scratch,
        compiler_params=pltpu.CompilerParams(vmem_limit_bytes=16 << 20),
    )


def lane_of(rows):
    return lax.broadcasted_iota(jnp.int32, (rows, LANES), 1)


def layer_norm(values, gain, axis):
    mean = jnp.mean(values, axis=axis, keepdims=True)
    centred = values - mean
    var = jnp.mean(centred * centred, axis=axis, keepdims=True)
    return centred * lax.rsqrt(var + EPS) * gain


def sigmoid(values):
    return 0.5 * jnp.tanh(0.5 * values) + 0.5


def normalize(block, gain, normed):
    pad = jnp.zeros((SLOT - SIDE, LANES), BF16)
    share = jnp.full((LANES, LANES), 1 / LANES, BF16)
    tokens = block[...].reshape(SIDE * SIDE, LANES)
    centred = tokens.astype(F32) - jnp.dot(tokens, share, preferred_element_type=F32)
    var = jnp.mean(centred * centred, axis=1, keepdims=True)
    rows = (centred * lax.rsqrt(var + EPS) * gain).astype(BF16)
    for i in range(SIDE):
        base = place_of(i)
        normed[base : base + SIDE, :] = rows[i * SIDE : (i + 1) * SIDE]
        normed[base + SIDE : base + SLOT, :] = pad


def place_of(i):
    return (i % HALF) * LANES + (i // HALF) * SLOT


def project(normed, weight, staged, extra):
    wt = (0.5 * weight.astype(F32)).T.astype(BF16)
    lane = lane_of(CH)
    for s in ORDER:
        proj = lax.dot_general(wt, normed[s * LANES : (s + 1) * LANES, :], NT, preferred_element_type=F32)
        left = (jnp.tanh(proj[:CH]) + 1.0) * proj[CH : 2 * CH]
        right = (jnp.tanh(proj[2 * CH : 3 * CH]) + 1.0) * proj[3 * CH :]
        first = jnp.where(lane < SLOT, left, pltpu.roll(right, SLOT, 1))
        second = jnp.where(lane < SLOT, pltpu.roll(left, SLOT, 1), right)
        if s + HALF >= MAIN:
            for g in range(SIDE // PIECE):
                extra[g * EXTRA + s + HALF - MAIN] = pltpu.roll(second, SIDE - g * PIECE, 1)
        else:
            staged[pl.ds((s + HALF) * STRIDE, CH), :] = jnp.where(lane % SLOT < SIDE, second, extra[s + HALF])
        staged[pl.ds(s * STRIDE, CH), :] = jnp.where(lane % SLOT < SIDE, first, extra[s])


ORDER = [*range(HALF - EXTRA, HALF), *range(HALF - EXTRA)]


def write_messages(staged, out):
    for channel in range(CH):
        for t in range(TILES):
            tile = staged[pl.ds(channel + t * TILE * STRIDE, TILE, stride=STRIDE), :]
            out[channel, :, t * LANES : (t + 1) * LANES] = tile.astype(BF16)


def project_kernel(pair_hbm, gain_hbm, weight_hbm, out, pair, gain, weight, sems, normed, staged, extra):
    places = ((gain_hbm, gain), (pair_hbm, pair), (weight_hbm.at[0], weight))
    copies = [pltpu.make_async_copy(source, target, sems.at[n]) for n, (source, target) in enumerate(places)]
    for copy in copies:
        copy.start()
    for copy in copies:
        copy.wait()
    normalize(pair, gain[0:1, :], normed)
    project(normed, weight[...], staged, extra)
    write_messages(staged, out)


def gate_kernel(p, pair, gain, gweight, gate, normed):
    normalize(pair, gain[p : p + 1, :], normed)
    for start in range(0, HALF * LANES, 4 * LANES):
        rows = slice(start, start + 4 * LANES)
        gate[rows, :] = sigmoid(jnp.dot(normed[rows, :], gweight[p], preferred_element_type=F32))


def read_sums(mixed, mixed32):
    for channel in range(CH):
        for t in range(KEPT // 2):
            tile = mixed[channel, :, t * LANES : (t + 1) * LANES].astype(F32)
            mixed32[pl.ds(channel * HALF + 2 * t, 2), :] = tile


def sums_of(mixed32, s):
    if s < KEPT:
        return mixed32[pl.ds(s, CH, stride=HALF), :]
    lane, sums = lane_of(CH) % SLOT, None
    for g in range(SIDE // PIECE):
        part = mixed32[pl.ds(g * (HALF - KEPT) + s - KEPT, CH, stride=HALF), :]
        part = pltpu.roll(part, LANES - SIDE + g * PIECE, 1)
        sums = part if sums is None else jnp.where(lane < g * PIECE, sums, part)
    return sums


def finish(pair, gate, mixed, hgain, oweight, z_out, mixed32, hidden, ready=lambda s: None):
    hcol = hgain.T
    read_sums(mixed, mixed32)
    for s in range(0, HALF, 4):
        sums = [sums_of(mixed32, s + t) for t in range(4)]
        sums = [layer_norm(values, hcol, 0).astype(BF16) for values in sums]
        for t in range(4):
            hidden[s + t] = sums[t]
    for s in range(0, HALF, 4):
        updates = [
            lax.dot_general(hidden[s + t], oweight, TN, preferred_element_type=F32) for t in range(4)
        ]
        change = gate[s * LANES : (s + 4) * LANES, :] * jnp.concatenate(updates, axis=0)
        for h in range(2):
            old = [pair[s + t + h * HALF].astype(F32) for t in range(4)]
            new = [
                old[t] + change[t * LANES + h * SLOT : t * LANES + h * SLOT + SIDE] for t in range(4)
            ]
            for t in range(4):
                z_out[s + t + h * HALF] = new[t].astype(BF16)
        ready(s + 4)


def middle_kernel(
    pair, gate, mixed, gain, hgain, oweight, weight, z_out, out, normed, mixed32, hidden, staged, extra
):
    finish(pair, gate, mixed, hgain[0:1, :], oweight[0], z_out, mixed32, hidden)
    normalize(z_out, gain[1:2, :], normed)
    project(normed, weight[1], staged, extra)
    write_messages(staged, out)


def last_kernel(pair, gate, mixed, hgain, oweight, z_hbm, z_out, sems, mixed32, hidden):
    copies = []

    def ready(s):
        for start in (s - HALF // 2, s + HALF // 2) if s % (HALF // 2) == 0 else ():
            rows = pl.ds(start, HALF // 2)
            copies.append(pltpu.make_async_copy(z_out.at[rows], z_hbm.at[rows], sems.at[len(copies)]))
            copies[-1].start()

    finish(pair, gate, mixed, hgain[1:2, :], oweight[1], z_out, mixed32, hidden, ready)
    for copy in copies:
        copy.wait()


def moved(got, p, base, offset):
    values = got[p].astype(F32)
    tiles = [values[:, t * LANES : (t + 1) * LANES] for t in range(TILES)]
    main = rolled(jnp.concatenate(tiles, axis=0), offset - base)
    first = rest = None
    for g in range(SIDE // PIECE):
        begin = offset + g * PIECE
        shift = begin - base - SIDE
        head = rolled(tiles[3 * g], shift)
        tail = rolled(jnp.concatenate(tiles[3 * g + 1 : 3 * g + 3], axis=0), shift)
        if g == 0:
            first, rest = head, tail
        else:
            first = jnp.where((lane_of(TILE) - begin) % LANES < PIECE, head, first)
            rest = jnp.where((lane_of(2 * TILE) - begin) % LANES < PIECE, tail, rest)
    return jnp.concatenate([main, first, rest], axis=0)


def rolled(values, shift):
    return pltpu.roll(values, shift % LANES, 1) if shift % LANES else values


def dense(ref, which, base):
    lane = lane_of(SIDE)
    tiles = [None] * 3
    for b, p in enumerate(which):
        first, offset = divmod(b * SIDE, LANES)
        block = moved(ref, p, base, offset)
        tiles[first] = block if offset == 0 else jnp.where(lane < offset, tiles[first], block)
        if offset + SIDE > LANES:
            tiles[first + 1] = block
    return jnp.concatenate(tiles, axis=1).astype(BF16)


def out_right_kernel(got, me, right):
    for a in range(4):
        for n, core in enumerate((me[0], 1 - me[0])):
            start = n * 192 + a * SIDE
            right[start : start + SIDE, :] = dense(got, [(2 * a + core) * 8 + b for b in range(8)], SLOT)


def out_left_kernel(got, left):
    for a in range(8):
        left[a * SIDE : (a + 1) * SIDE, :] = dense(got, [a * 8 + b for b in range(8)], 0)


def send_back(total, blocks, place, out):
    lane = lane_of(HALF)
    for a in range(blocks):
        for b in range(0, 4, 2):
            tile = total[a * SIDE : (a + 1) * SIDE, b * SLOT : (b + 2) * SLOT]
            low, high = tile[:HALF], tile[HALF:]
            write_sums(jnp.where(lane < SLOT, low, pltpu.roll(high, SLOT, 1)), place(a, b), out)
            write_sums(jnp.where(lane < SLOT, pltpu.roll(low, SLOT, 1), high), place(a, b + 1), out)


def write_sums(rows, p, out):
    last = rows[16:]
    spare = [pltpu.roll(last, SIDE - g * PIECE, 1)[KEPT - 16 :] for g in range(SIDE // PIECE)]
    lane = lane_of(KEPT) % SLOT
    rows = jnp.where(lane < SIDE, rows[:KEPT], jnp.concatenate(spare, axis=0))
    for t in range(KEPT // 2):
        out[p, :, t * LANES : (t + 1) * LANES] = rows[2 * t : 2 * t + 2].astype(BF16)


def padded(ref, start):
    pad = jnp.zeros((SLOT - SIDE, ref.shape[1]), BF16)
    pieces = []
    for b in range(4):
        pieces += [ref[start + b * SIDE : start + (b + 1) * SIDE, :], pad]
    return jnp.concatenate(pieces, axis=0)


def out_sums(left, left_c, near, far, place, out):
    total = lax.dot_general(left[...], padded(near, 0), NT, preferred_element_type=F32)
    total += lax.dot_general(left_c[...], padded(far, 192), NT, preferred_element_type=F32)
    send_back(total, 8, place, out)


def out_early_kernel(left, left_c, right, right_c, out):
    out_sums(left, left_c, right, right_c, lambda a, b: a * 4 + b, out)


def out_late_kernel(left, left_c, right_y, right_yc, early, me, out):
    def place(owner):
        return lambda a, b: a * 8 + (2 * (b // 2) + owner) * 2 + b % 2

    for a in range(8):
        for b in range(4):
            out[place(me[0])(a, b)] = early[a * 4 + b]
    out_sums(left, left_c, right_y, right_yc, place(1 - me[0]), out)


def in_left_kernel(got, out, left):
    for r in range(8):
        rows = slice(r * SIDE, (r + 1) * SIDE)
        left[rows, :] = dense(got, [(r + 8 * h) * 4 + b for h in range(2) for b in range(4)], 0)
    out[...] = left[...].T


def in_right_kernel(got, right):
    lane = lane_of(SIDE)
    for r in range(16):
        for b in range(0, 4, 2):
            low, high = moved(got, r * 4 + b, SLOT, 0), moved(got, r * 4 + b + 1, SLOT, SLOT)
            tile = jnp.where(lane < SLOT, low, high)
            right[r * SIDE : (r + 1) * SIDE, b * SLOT : (b + 2) * SLOT] = tile.astype(BF16)


def in_sums(left, right, place, out):
    total = jnp.dot(left[:192, :], right[:384, :], preferred_element_type=F32)
    total += jnp.dot(left[192:, :], right[384:, :], preferred_element_type=F32)
    send_back(total, 4, place, out)


def in_early_kernel(right, left, left_c, left_x, out):
    for n, ref in enumerate((left, left_c, left_x)):
        in_sums(ref, right, lambda a, b: n * 16 + a * 4 + b, out)


def in_late_kernel(right, left_d, early, me, core, out):
    def place(low, c):
        return lambda a, b: (2 * (a // 2) + low) * 16 + (2 * (a % 2) + c) * 4 + b

    places = [(me[0], core[0]), (me[0], 1 - core[0]), (1 - me[0], core[0])]
    for n, at in enumerate(places):
        for a in range(4):
            for b in range(4):
                out[place(*at)(a, b)] = early[n * 16 + a * 4 + b]
    in_sums(left_d, right, place(1 - me[0], 1 - core[0]), out)


def swap(values, *axes):
    n = 1 << len(axes)
    return lax.ppermute(values, axes, [(i, n - 1 - i) for i in range(n)])


MESSAGE = (CH, TILE, TILES * LANES)
EXTRAS = (MAIN, CH, LANES)
BACK = (CH, 2, KEPT // 2 * LANES)
BLOCK = (SIDE, SIDE, LANES)
GATE = (HALF * LANES, LANES)


def body(pair, norm_gain, proj_weight, hid_gain, out_weight, gate_weight):
    normed = pltpu.VMEM(GATE, BF16)
    staged = pltpu.VMEM(((MAIN + 1) * STRIDE, LANES), F32)
    extra = pltpu.VMEM(EXTRAS, F32)
    mixed32 = pltpu.VMEM(((CH + 1) * HALF, LANES), F32)
    hidden = pltpu.VMEM((HALF, CH, LANES), BF16)
    block = pltpu.VMEM(BLOCK, BF16)
    gain32, weight = pltpu.VMEM((2, LANES), F32), pltpu.VMEM((LANES, 4 * CH), BF16)
    out_axes, in_axes = ("yh", "zl", "xh", "xl", "zh"), ("yh", "yl", "zl", "xh", "zh")
    tie = lax.optimization_barrier
    pair, core, low_y, low_x = tie((pair, *(lax.axis_index(name).reshape(1) for name in ("c", "yl", "xl"))))

    (sent,) = call(
        project_kernel,
        [MESSAGE],
        3,
        [block, gain32, weight, pltpu.SemaphoreType.DMA((3,)), normed, staged, extra],
        inputs=HBM,
        pin=True,
    )(*(pltpu.with_memory_space_constraint(x, pltpu.HBM) for x in (pair, norm_gain, proj_weight)))
    got = lax.all_to_all(sent, out_axes, 0, 0, tiled=True)
    (right,) = call(out_right_kernel, [(384, 384)], 1, smem=1)(got, core)
    right_y, right_c = swap(right, "yl"), swap(right, "c")
    got, right = tie((got, right))
    (left,) = call(out_left_kernel, [(384, 384)], 1)(got)
    left_c = swap(left, "c")
    source, left = tie((pair, left))
    (gate,) = call(functools.partial(gate_kernel, 0), [GATE], 3, [normed], dtype=F32)(source, norm_gain, gate_weight)
    right_y, gate, left = tie((right_y, gate, left))
    (early,) = call(out_early_kernel, [(32, *BACK[1:])], 4)(left, left_c, right, right_c)
    (sent,) = call(out_late_kernel, [BACK], 5, smem=1)(
        left, left_c, right_y, swap(right_y, "c"), early, low_y
    )
    mixed = lax.all_to_all(sent, out_axes, 0, 0, tiled=True)
    first, sent = call(middle_kernel, [BLOCK, MESSAGE], 7, [normed, mixed32, hidden, staged, extra])(
        pair, gate, mixed, norm_gain, hid_gain, out_weight, proj_weight
    )
    got = lax.all_to_all(sent, in_axes, 0, 0, tiled=True)
    (left,) = call(in_left_kernel, [(384, 384)], 1, [pltpu.VMEM((384, 384), BF16)])(got)
    left_x, left_c = swap(left, "xl"), swap(left, "c")
    got, left = tie((got, left))
    (right,) = call(in_right_kernel, [(768, 256)], 1)(got)
    source, right = tie((first, right))
    (gate,) = call(functools.partial(gate_kernel, 1), [GATE], 3, [normed], dtype=F32)(source, norm_gain, gate_weight)
    left_x, gate, right = tie((left_x, gate, right))
    (early,) = call(in_early_kernel, [(48, *BACK[1:])], 4)(right, left, left_c, left_x)
    (sent,) = call(in_late_kernel, [BACK], 3, smem=2)(right, swap(left_x, "c"), early, low_x, core)
    mixed = lax.all_to_all(sent, in_axes, 0, 0, tiled=True)
    (updated,) = call(
        last_kernel,
        [BLOCK],
        5,
        [block, pltpu.SemaphoreType.DMA((4,)), mixed32, hidden],
        outputs=HBM,
    )(first, gate, mixed, hid_gain, out_weight)
    return updated


def solution(mesh):
    names = ("yh", "yl", "zl", "xh", "xl", "zh", "c")
    fine = Mesh(mesh.devices.reshape(2, 2, 4, 2, 2, 2, 2), names)
    spec = P(names[:3], names[3:], None)
    return jax.shard_map(
        body,
        mesh=fine,
        in_specs=(spec, P(), P(), P(), P(), P()),
        out_specs=spec,
        check_vma=False,
    )
```
